256 devices in a mesh: ctx: 32 (over z, y_hi, core), head: 8 (over y_lo, x).
Axes of the slice: x: 4, y: 4 (y_hi: 2, y_lo: 2; y = y_hi * 2 + y_lo), z: 8, core: 2. Of those that a mesh axis runs over, the one named last changes fastest.
Arguments:
- latents: bfloat16 [16384, 4096], P('ctx', 'head')
- norm_gain: bfloat16 [4096], P('head'), may hold values from 0.5 to 2
- w_qkv: bfloat16 [4096, 32, 384], P('ctx', 'head')
- source_unit: int32 [512], replicated, may hold values from 0 to 511, as said below
- first_block: int32 [1], replicated, may hold values from 0 to 31
Outputs:
- attended: bfloat16 [16384, 32, 128], P('ctx', 'head')
The draws below stay inside these ranges and needn't reach their ends.
Inputs may be any that keep to these rules, and one draw needn't show every extreme that they name: `source_unit`: A permutation of the 512 units. The 16 units of the sequence that one block of 512 rows holds come from 16 different encoder blocks, so one encoder block gives at most one unit to one sequence block.
All inputs are finite; a program needn't handle non-finite values.
Results may differ from the reference program's by a relative error of at most 0.0094.
Values may be sent and summed in bfloat16 or wider, within the bound.
A program may use at most 128 MiB of HBM per device.

```python
import math
import jax
import jax.numpy as jnp
from jax import lax

D = 4096
HEADS = 32
HEAD_DIM = 128
TOK_DEV = 512
UNITS_DEV = 16
STEPS = 4
TOKENS = 16384
UNITS = 512
N_CTX = 32


def draw_latents(key, part):
    key = jax.random.fold_in(key, 7)
    first_key = jax.random.fold_in(key, 0)
    base = jax.random.normal(first_key, (TOKENS, D), jnp.float32)
    return base.astype(jnp.bfloat16)


def draw_w_qkv(key, part):
    key = jax.random.fold_in(key, 5)
    first_key = jax.random.fold_in(key, 0)
    base = jax.random.normal(first_key, (D, HEADS, 3 * HEAD_DIM), jnp.float32) * D ** (-0.5)
    return base.astype(jnp.bfloat16)


def draw_source_unit(key, part):
    key = jax.random.fold_in(key, 11)
    key_one, key_two, key_three, key_four = jax.random.split(key, 4)
    relabel = jax.random.permutation(key_one, N_CTX)
    inverse = jnp.argsort(relabel)
    shifts = jax.random.permutation(key_two, N_CTX)[:UNITS_DEV]
    src_dev = relabel[(inverse[:, None] + shifts[None, :]) % N_CTX]
    orders = jax.vmap(lambda sub: jax.random.permutation(sub, UNITS_DEV))(jax.random.split(key_three, N_CTX))
    slot_index = jnp.broadcast_to(jnp.arange(UNITS_DEV, dtype=jnp.int32)[None, :], (N_CTX, UNITS_DEV))
    local_unit = orders[src_dev, slot_index]
    global_unit = (src_dev * UNITS_DEV + local_unit).astype(jnp.int32)
    shuffles = jax.vmap(lambda sub: jax.random.permutation(sub, UNITS_DEV))(jax.random.split(key_four, N_CTX))
    placed = jnp.take_along_axis(global_unit, shuffles, axis=1)
    return placed.reshape(UNITS).astype(jnp.int32)


def block_levels(key, shape, shards, smallest, high):
    loudness, own = 1.0, jax.random.fold_in(key, 6)
    for axis_at, blocks in shards:
        steps = jnp.exp(jax.random.uniform(jax.random.fold_in(own, axis_at), (blocks,), jnp.float32, smallest / len(shards), high / len(shards)))
        loudness = loudness * jnp.repeat(steps, shape[axis_at] // blocks).reshape([-1 if axis == axis_at else 1 for axis in range(len(shape))])
    return loudness


def setup_inputs(seed: int = 0) -> dict:
    seeds = jax.random.split(jax.random.key(seed), 6)
    latents = draw_latents(jax.random.fold_in(seeds[5], 71), 0)
    norm_gain = jnp.clip(jnp.exp(math.log(2.0) - 1.3862944 * jax.random.uniform(seeds[1], (D,), jnp.float32) ** block_levels(seeds[1], (D,), ((0, 8),), -0.2, 0.2)), 0.5, 2.0).astype(jnp.bfloat16)
    w_qkv = draw_w_qkv(jax.random.fold_in(seeds[5], 71), 0)
    source_unit = draw_source_unit(jax.random.fold_in(seeds[5], 71), 0)
    first_block = jax.random.randint(seeds[4], (1,), 0, N_CTX).astype(jnp.int32)
    return dict(latents=latents, norm_gain=norm_gain, w_qkv=w_qkv, source_unit=source_unit, first_block=first_block)


EPS = 1e-05
ROPE_BASE = 50000000.0

def rope_tables(positions):
    half = HEAD_DIM // 2
    freq = jnp.exp(-math.log(ROPE_BASE) * jnp.arange(half, dtype=jnp.float32) * (2.0 / HEAD_DIM))
    angles = positions.astype(jnp.float32)[:, None] * freq[None, :]
    return (jnp.cos(angles), jnp.sin(angles))

def rotate(values_in, cosine, sine):
    half = values_in.shape[-1] // 2
    left = values_in[..., :half]
    right = values_in[..., half:]
    cos_b = cosine[:, None, :]
    sin_b = sine[:, None, :]
    return jnp.concatenate([left * cos_b - right * sin_b, right * cos_b + left * sin_b], -1)

def reference(latents, norm_gain, w_qkv, source_unit, first_block):
    unit = TOK_DEV // UNITS_DEV
    units = latents.reshape(UNITS, unit, D)
    seq = jnp.take(units, source_unit, axis=0).reshape(N_CTX, TOK_DEV, D)
    w_flat = w_qkv.reshape(D, HEADS * 3 * HEAD_DIM)
    opening = first_block[0]
    gain = norm_gain.astype(jnp.float32)

    def project(args):
        rows, index = args
        rows_f = rows.astype(jnp.float32)
        scale = lax.rsqrt(lax.optimization_barrier(jnp.mean(rows_f * rows_f, -1, keepdims=True)) + EPS)
        normed = (rows_f * scale * gain).astype(jnp.bfloat16)
        qkv = jnp.dot(normed, w_flat, preferred_element_type=jnp.float32).reshape(TOK_DEV, HEADS, 3 * HEAD_DIM)
        block = (index - opening) % N_CTX
        positions = block * TOK_DEV + jnp.arange(TOK_DEV, dtype=jnp.int32)
        cosine, sine = rope_tables(positions)
        query = rotate(qkv[..., :HEAD_DIM], cosine, sine).astype(jnp.bfloat16)
        keys = rotate(qkv[..., HEAD_DIM:2 * HEAD_DIM], cosine, sine).astype(jnp.bfloat16)
        values = qkv[..., 2 * HEAD_DIM:].astype(jnp.bfloat16)
        return (query, jnp.concatenate([keys, values], -1))
    query_all, pairs = lax.map(project, (seq, jnp.arange(N_CTX, dtype=jnp.int32)))

    def attend(index):
        block = (index - opening) % N_CTX
        query = lax.dynamic_index_in_dim(query_all, index, 0, keepdims=False)
        parts = []
        for lag in reversed(range(STEPS)):
            source = ((index - lag) % N_CTX).astype(jnp.int32)
            parts.append(lax.dynamic_index_in_dim(pairs, source, 0, keepdims=False))
        joined = jnp.concatenate(parts, 0)
        keys = joined[..., :HEAD_DIM]
        values = joined[..., HEAD_DIM:]
        slot = jnp.arange(STEPS * TOK_DEV, dtype=jnp.int32)
        key_pos = (block - (STEPS - 1) + slot // TOK_DEV) * TOK_DEV + slot % TOK_DEV
        query_pos = block * TOK_DEV + jnp.arange(TOK_DEV, dtype=jnp.int32)
        allowed = (key_pos[None, :] >= 0) & (key_pos[None, :] <= query_pos[:, None])
        scores = jnp.einsum('qhe,khe->hqk', query.astype(jnp.float32), keys.astype(jnp.float32)) * HEAD_DIM ** (-0.5)
        scores = jnp.where(allowed[None], scores, jnp.float32(-1e+30))
        peak = lax.optimization_barrier(jnp.max(scores, -1, keepdims=True))
        weights = jnp.where(allowed[None], jnp.exp(scores - peak), jnp.float32(0.0))
        total = lax.optimization_barrier(jnp.sum(weights, -1))
        rounded = lax.optimization_barrier(weights.astype(jnp.bfloat16)).astype(jnp.float32)
        summed = jnp.einsum('hqk,khe->qhe', rounded, values.astype(jnp.float32))
        return (summed / jnp.transpose(total)[:, :, None]).astype(jnp.bfloat16)
    attended = lax.map(attend, jnp.arange(N_CTX, dtype=jnp.int32))
    return attended.reshape(TOKENS, HEADS, HEAD_DIM)
```

```python
import math

import jax
import jax.numpy as jnp
from jax import lax
from jax.experimental import pallas as pl
from jax.experimental.pallas import tpu as pltpu
from jax.sharding import PartitionSpec as P

HEAD_DIM = 128
UNITS_DEV = 16
STEPS = 4
EPS = 1e-05
ROPE_BASE = 50000000.0

BLOCK = 512
UNIT = BLOCK // UNITS_DEV
SLICE = 512
PART = 256
NZ, NY, NX = 8, 4, 4
CYCLE = 32
WIDTH = 4096
MESH = pl.DeviceIdType.MESH
F32, BF16 = jnp.float32, jnp.bfloat16
DELTA = (0, -1, 1, 2)


def kernel(
    pick_ref, slot_ref, bias_ref, lat_ref, gain_ref, w_ref, cos_ref, sin_ref, out_ref,
    sbuf, rbuf_0, rbuf_1, xg, own_sum, all_sums, normed, wstage_kv, wstage_q, wkv, wq, acc_kv, acc_q, kvb, qb, att, mrow, lrow, obuf, oswap,
    a_send, a_recv, g_send, g_recv, x_send, x_recv, y_send, y_recv, z_send, z_recv, c_send, c_recv, h_send, h_recv,
    o_send, o_recv,
):
    ctx, head = lax.axis_index("ctx"), lax.axis_index("head")
    z, yh, c = ctx // 4, (ctx // 2) % 2, ctx % 2
    yl, x = head // 4, head % 4
    y = yh * 2 + yl

    def place(at_x, at_y):
        at_x, at_y = lax.rem(at_x + 4, 4), lax.rem(at_y + 4, 4)
        return at_y // 2, lax.rem(at_y, 2) * 4 + at_x

    def device(at_x, at_y, at_z, at_c):
        row, column = place(at_x, at_y)
        return (lax.rem(at_z + NZ, NZ) * 4 + row * 2 + at_c, column)

    right, left = device(x + 1, y, z, c), device(x - 1, y, z, c)
    up, down = device(x, y + 1, z, c), device(x, y - 1, z, c)
    above, below = device(x, y, z + 1, c), device(x, y, z - 1, c)
    sibling = device(x, y, z, 1 - c)
    partner = device(x, y + 2, z, c)

    def copy(src, dst, send, recv, to):
        return pltpu.make_async_remote_copy(
            src_ref=src, dst_ref=dst, send_sem=send, recv_sem=recv, device_id=to, device_id_type=MESH
        )

    barrier = pltpu.get_barrier_semaphore()

    @pl.loop(1, CYCLE)
    def _(step):
        pl.semaphore_signal(barrier, inc=1, device_id=(lax.rem(ctx + step, CYCLE), head), device_id_type=MESH)

    @pl.loop(1, 8)
    def _(step):
        pl.semaphore_signal(barrier, inc=1, device_id=(ctx, lax.rem(head + step, 8)), device_id_type=MESH)

    for to in (up, down):
        pl.semaphore_signal(barrier, inc=1, device_id=to, device_id_type=MESH)

    eye = lax.broadcasted_iota(jnp.int32, (128, 128), 0) == lax.broadcasted_iota(jnp.int32, (128, 128), 1)
    for at in range(4):
        rows = lat_ref[at * 128 : (at + 1) * 128].astype(F32)
        sums = jnp.sum(rows * rows, -1, keepdims=True)
        own_sum[:, at * 128 : (at + 1) * 128] = jnp.sum(jnp.where(eye, sums, 0.0), 0, keepdims=True)
    all_sums[head] = own_sum[...]
    for at in range(4):
        pair, side = at // 2, at % 2
        start = at * 384
        wstage_q[pair, :, side * 128 : (side + 1) * 128] = w_ref[:, start : start + 128]
        wstage_kv[pair, :, side * 128 : (side + 1) * 128] = w_ref[:, start + 128 : start + 256]
        wstage_kv[pair, :, 256 + side * 128 : 256 + (side + 1) * 128] = w_ref[:, start + 256 : start + 384]

    pl.semaphore_wait(barrier, CYCLE - 1 + 7 + 2)

    def sum_copy(step):
        return copy(
            own_sum, all_sums.at[head], g_send.at[step], g_recv.at[head], (ctx, lax.rem(head + step, 8))
        )

    def sum_arrival(step):
        origin = lax.rem(head + step, 8)
        return copy(own_sum, all_sums.at[origin], g_send.at[step], g_recv.at[origin], (ctx, origin))

    @pl.loop(1, 8)
    def _(step):
        sum_copy(step).start()

    stages, weights = (wstage_kv, wstage_q), (wkv, wq)

    def swap_copy(kind, row):
        return copy(
            stages[kind].at[1 - row], weights[kind].at[z, c, row], y_send.at[kind], y_recv.at[kind], partner
        )

    for kind in range(2):
        swap_copy(kind, yh).start()
        weights[kind][z, c, yh] = stages[kind][yh]

    rbuf = (rbuf_0, rbuf_1)

    def unit_copy(part, step):
        return copy(
            sbuf.at[part, step], rbuf[part].at[step], a_send.at[part], a_recv.at[part],
            (lax.rem(ctx + step, CYCLE), head),
        )

    @pl.loop(1, 8)
    def _(step):
        sum_arrival(step).wait_recv()

    total = jnp.sum(all_sums[...], 0)
    inverse = lax.rsqrt(total / WIDTH + EPS)
    gain = gain_ref[0:1].astype(F32)
    for at in range(4):
        across = jnp.broadcast_to(inverse[:, at * 128 : (at + 1) * 128], (128, 128))
        scale = jnp.sum(jnp.where(eye, across, 0.0), -1, keepdims=True)
        rows = slice(at * 128, (at + 1) * 128)
        value = (lat_ref[rows].astype(F32) * scale * gain).astype(BF16)
        normed[at * 4 : (at + 1) * 4] = value.reshape(4, UNIT, SLICE)

    for part in range(2):

        @pl.loop(0, CYCLE)
        def _(step, part=part):
            sbuf[part, step] = normed[pick_ref[step], :, part * PART : (part + 1) * PART]

        @pl.loop(1, CYCLE // 2)
        def _(step, part=part):
            unit_copy(part, step).start()
            unit_copy(part, CYCLE - step).start()

        unit_copy(part, CYCLE // 2).start()

    def x_region(part, half, first, second, quarter=None):
        at = place(first, second) if half == 0 else place(second, first)
        start, size = half * 256, 256
        if quarter is not None:
            start, size = start + quarter * 128, 128
        return xg.at[part, at[0], at[1], pl.ds(start, size), :]

    me_at = ((x, y), (y, x))
    ways = (((right, left), (up, down)), ((up, down), (right, left)))

    def x_copy(part, half, stage, s, way, receive=False):
        first, second = me_at[half]
        back = (-1 if way == 0 else 1) * (1 if receive else 0)
        on = -1 if way == 0 else 1
        if stage == 0:
            region, axis = x_region(part, half, first + back, second), 0
        elif stage == 1:
            region, axis = x_region(part, half, first + on + back, second, way), 0
        elif stage == 2:
            region, axis = x_region(part, half, first + DELTA[s], second + back), 1
        else:
            region, axis = x_region(part, half, first + DELTA[s], second + on + back, way), 1
        sem = (0, 2, 4, 12)[stage] + s * 2 + way
        return copy(
            region, region, x_send.at[part, half, sem], x_recv.at[part, half, sem], ways[half][axis][way]
        )

    def x_start(part, stage, s, way):
        for half in range(2):
            x_copy(part, half, stage, s, way).start()

    def x_wait(part, half, stage, s, way):
        x_copy(part, half, stage, s, way, receive=True).wait_recv()

    def arrange(part):
        rbuf[part][0] = sbuf[part, 0]
        copy(
            sbuf.at[part, pl.ds(1, CYCLE - 1)], rbuf[part].at[pl.ds(1, CYCLE - 1)], a_send.at[part], a_recv.at[part],
            sibling,
        ).wait_recv()
        for unit in range(UNITS_DEV):
            xg[part, yh, head, unit * UNIT : (unit + 1) * UNIT, :] = rbuf[part][slot_ref[unit]]

    def begin(part):
        for stage in (0, 2):
            for way in range(2):
                x_start(part, stage, 0, way)

    def first_axis(part):
        for way in range(2):
            for half in range(2):
                x_wait(part, half, 0, 0, way)
                x_copy(part, half, 1, 0, way).start()
        for s in (1, 2):
            for way in range(2):
                x_start(part, 2, s, way)

    def first_axis_end(part):
        for half in range(2):
            for way in range(2):
                x_wait(part, half, 1, 0, way)
        for way in range(2):
            x_start(part, 2, 3, way)

    def second_axis(part, s):
        for way in range(2):
            for half in range(2):
                x_wait(part, half, 2, s, way)
                x_copy(part, half, 3, s, way).start()

    def second_axis_end(part):
        for s in range(4):
            for half in range(2):
                for way in range(2):
                    x_wait(part, half, 3, s, way)

    def w_region(kind, at_z, row=None):
        at_z = lax.rem(at_z + NZ, NZ)
        return weights[kind].at[at_z, c] if row is None else weights[kind].at[at_z, c, row]

    def w_copy(kind, hop, way, receive=False):
        on = (-1 if way == 0 else 1) * (hop if receive else hop - 1)
        region = w_region(kind, z + on, None if hop < 4 else way)
        sem = (hop - 1) * 2 + way
        return copy(region, region, z_send.at[kind, sem], z_recv.at[kind, sem], (above, below)[way])

    def w_share(kind, at, receive=False):
        at_z = lax.rem(z + at, NZ)
        core = 1 - c if receive else c
        region = weights[kind].at[at_z, core]
        return copy(region, region, c_send.at[kind, at], c_recv.at[kind, at], sibling)

    def w_hop(kind, hop):
        if hop == 1:
            swap_copy(kind, 1 - yh).wait_recv()
            for way in range(2):
                w_copy(kind, 1, way).start()
            w_share(kind, 0).start()
            return
        for way in range(2):
            w_copy(kind, hop - 1, way, receive=True).wait_recv()
            if hop <= 4:
                w_copy(kind, hop, way).start()
            if hop - 1 < 4:
                w_share(kind, (NZ - (hop - 1)) if way == 0 else hop - 1).start()
        if hop == 5:
            w_share(kind, 4).start()

    arrange(0)
    begin(0)
    w_hop(0, 1)
    first_axis(0)
    first_axis_end(0)
    w_hop(0, 2)
    w_hop(1, 1)
    second_axis(0, 0)
    second_axis(0, 1)
    arrange(1)
    begin(1)
    w_hop(0, 3)
    second_axis(0, 2)
    second_axis(0, 3)
    w_hop(1, 2)
    first_axis(1)
    w_hop(0, 4)
    first_axis_end(1)
    w_hop(1, 3)
    second_axis_end(0)
    second_axis(1, 0)
    w_hop(0, 5)
    second_axis(1, 1)
    w_hop(1, 4)
    second_axis(1, 2)
    second_axis(1, 3)

    def project(kind, part, row):
        acc = (acc_kv, acc_q)[kind]

        def one(k):
            w_rows = jnp.concatenate([weights[kind][k, 0, part], weights[kind][k, 1, part]], 0)
            return jnp.dot(xg[part, row, k], w_rows, preferred_element_type=F32)

        if part == 0:
            acc[row] = one(0)
        else:
            acc[row] += one(0)

        @pl.loop(1, 8)
        def _(k):
            acc[row] += one(k)

    for at in range(8):
        w_share(0, at, receive=True).wait_recv()
    for row in range(2):
        project(0, 0, row)
    w_hop(1, 5)
    second_axis_end(1)

    def turn(value, row):
        return value * cos_ref[row] + pltpu.roll(value, HEAD_DIM // 2, 1) * sin_ref[row]

    def kv_region(at, side):
        return kvb.at[at, side]

    def halo(which, side, receive=False):
        if which == 0:
            src, dst, to = 5 + c, 1 + c, above
        elif which == 1:
            src, dst, to = 1 + c, 1 + c, sibling
            if receive:
                dst = 2 - c
        elif which == 2:
            src, dst, to = 3 + c, 3 + c, sibling
            if receive:
                dst = 4 - c
        elif which == 3:
            src, dst, to = 5, 5, sibling
        else:
            src, dst, to = 4, 0, device(x, y, z + 1, 0)
        return copy(kv_region(src, side), kv_region(dst, side), h_send.at[which, side], h_recv.at[which, side], to)

    for row in (1, 0):
        project(0, 1, row)
        for side in range(2):
            keys = acc_kv[row, :, side * 128 : (side + 1) * 128]
            vals = acc_kv[row, :, 256 + side * 128 : 256 + (side + 1) * 128]
            at = 2 * row + 3 + c
            kvb[at, side, 0] = turn(keys, row).astype(BF16)
            kvb[at, side, 1] = vals.astype(BF16)
            if row == 1:
                halo(0, side).start()

                @pl.when(c == 0)
                def _(side=side):
                    halo(3, side).start()

            else:

                @pl.when(c == 1)
                def _(side=side):
                    halo(4, side).start()

                halo(2, side).start()

    for at in range(8):
        w_share(1, at, receive=True).wait_recv()
    for row in (1, 0):
        project(1, 0, row)
        project(1, 1, row)
        for side in range(2):
            query = acc_q[row, :, side * 128 : (side + 1) * 128]
            qb[row, side] = turn(query, row).astype(BF16)

    def scores(query, at, side, size=BLOCK):
        keys = kvb[at, side, 0, :size]
        product = lax.dot_general(query, keys, (((1,), (1,)), ((), ())), preferred_element_type=F32)
        return product * (HEAD_DIM**-0.5 * math.log2(math.e))

    def attend(row, side, tile, lags, first):
        rows = pl.ds(tile * 256, 256)
        query = qb[row, side, rows]
        own = 2 * row + 3 + c
        pieces = []
        for lag in lags:
            if lag == 0:
                size = (tile + 1) * 256
                value = scores(query, own, side, size)
                seen = (
                    lax.broadcasted_iota(jnp.int32, (256, size), 0) + tile * 256
                    >= lax.broadcasted_iota(jnp.int32, (256, size), 1)
                )
                pieces.append((jnp.where(seen, value, -1e30), 0.0, own, size))
            else:
                pieces.append((scores(query, own - lag, side), bias_ref[row * STEPS + lag], own - lag, BLOCK))
        peak = None
        for value, bias, _, _ in pieces:
            top = jnp.max(value, -1, keepdims=True) + bias
            peak = top if peak is None else jnp.maximum(peak, top)
        if not first:
            before = mrow[row, side, rows, :1]
            peak = jnp.maximum(peak, before)
        total, summed = None, None
        for value, bias, at, size in pieces:
            weight = jnp.exp2(value - (peak - bias))
            part_total = jnp.sum(weight, -1, keepdims=True)
            part_sum = jnp.dot(weight.astype(BF16), kvb[at, side, 1, :size], preferred_element_type=F32)
            total = part_total if total is None else total + part_total
            summed = part_sum if summed is None else summed + part_sum
        if not first:
            keep = jnp.exp2(before - peak)
            total = total + lrow[row, side, rows, :1] * keep
            summed = summed + att[row, side, rows] * keep
        mrow[row, side, rows] = jnp.broadcast_to(peak, (256, 128))
        lrow[row, side, rows] = jnp.broadcast_to(total, (256, 128))
        att[row, side, rows] = summed

    def attend_all(row, side, lags, first=False):
        for tile in range(2):
            attend(row, side, tile, lags, first)

    for side in range(2):
        halo(2, side, receive=True).wait_recv()

        @pl.when(c == 1)
        def _(side=side):
            halo(3, side).wait_recv()

        attend_all(1, side, (0, 1, 2), True)
        attend_all(0, side, (0,), True)

    def pass_on(side):
        copy(
            kv_region(5 + c, side), kv_region(1 + c, side), h_send.at[0, side], h_recv.at[0, side], above
        ).wait_recv()
        halo(1, side).start()

    for side in range(2):
        pass_on(side)

    def finish(row, side):
        columns = slice(side * 128, (side + 1) * 128)
        obuf[row, :, columns] = (att[row, side] / lrow[row, side]).astype(BF16)

    def out_copy(row):
        return copy(obuf.at[1 - row], oswap, o_send.at[0], o_recv.at[0], partner)

    for side in range(2):
        halo(1, side, receive=True).wait_recv()
        attend_all(1, side, (3,))
        finish(1, side)

    @pl.when(yh == 0)
    def _():
        out_copy(0).start()

    for side in range(2):

        @pl.when(c == 0)
        def _(side=side):
            halo(4, side).wait_recv()

        attend_all(0, side, (1, 2, 3))
        finish(0, side)

    @pl.when(yh == 1)
    def _():
        out_copy(1).start()

    out_copy(yh).wait_recv()
    out_ref[yh] = obuf[yh]
    out_ref[1 - yh] = oswap[...]

    @pl.loop(1, 8)
    def _(step):
        sum_copy(step).wait_send()

    for part in range(2):
        copy(
            sbuf.at[part, pl.ds(1, CYCLE - 1)], rbuf[part].at[pl.ds(1, CYCLE - 1)], a_send.at[part], a_recv.at[part],
            sibling,
        ).wait_send()
        for half in range(2):
            for way in range(2):
                for stage in range(4):
                    for s in range(4 if stage >= 2 else 1):
                        x_copy(part, half, stage, s, way).wait_send()
    for kind in range(2):
        swap_copy(kind, yh).wait_send()
        for hop in range(1, 5):
            for way in range(2):
                w_copy(kind, hop, way).wait_send()
        for at in range(8):
            w_share(kind, at).wait_send()
    for side in range(2):
        for which in range(3):
            halo(which, side).wait_send()

        @pl.when(c == 0)
        def _(side=side):
            halo(3, side).wait_send()

        @pl.when(c == 1)
        def _(side=side):
            halo(4, side).wait_send()

    out_copy(yh).wait_send()


def per_device(latents, norm_gain, w_qkv, source_unit, first_block):
    own_index = lax.axis_index("ctx")
    table = source_unit.reshape(CYCLE, UNITS_DEV)
    owner = table // UNITS_DEV
    pick = jnp.sum(jnp.where(owner == own_index, table % UNITS_DEV, 0), axis=1)
    pick = jnp.take(pick, (own_index + jnp.arange(CYCLE, dtype=jnp.int32)) % CYCLE)
    slot = (own_index - lax.dynamic_index_in_dim(owner, own_index, 0, keepdims=False)) % CYCLE
    own_blocks = own_index // 4 * 4 + own_index % 2 + jnp.array([0, 2], jnp.int32)
    block = (own_blocks - first_block[0]) % CYCLE
    bias = jnp.where(block[:, None] >= jnp.arange(STEPS, dtype=jnp.int32)[None, :], 0.0, -1e30).astype(F32)
    half = HEAD_DIM // 2
    positions = block[:, None] * BLOCK + jnp.arange(BLOCK, dtype=jnp.int32)[None, :]
    freq = jnp.exp(-math.log(ROPE_BASE) * jnp.arange(half, dtype=F32) * (2.0 / HEAD_DIM))
    angles = positions.astype(F32)[..., None] * freq
    cosine, sine = jnp.cos(angles), jnp.sin(angles)
    cosine = jnp.concatenate([cosine, cosine], -1)
    sine = jnp.concatenate([-sine, sine], -1)
    smem, vmem = pl.BlockSpec(memory_space=pltpu.SMEM), pl.BlockSpec(memory_space=pltpu.VMEM)
    dma = pltpu.SemaphoreType.DMA
    out = pl.pallas_call(
        kernel,
        out_shape=jax.ShapeDtypeStruct((2, BLOCK, 256), BF16),
        in_specs=[smem] * 3 + [vmem] * 5,
        out_specs=vmem,
        scratch_shapes=[
            pltpu.VMEM((2, CYCLE, UNIT, PART), BF16),
            pltpu.VMEM((CYCLE, UNIT, PART), BF16),
            pltpu.VMEM((CYCLE, UNIT, PART), BF16),
            pltpu.VMEM((2, 2, 8, BLOCK, PART), BF16),
            pltpu.VMEM((1, BLOCK), F32),
            pltpu.VMEM((8, 1, BLOCK), F32),
            pltpu.VMEM((UNITS_DEV, UNIT, SLICE), BF16),
            pltpu.VMEM((2, 128, 512), BF16),
            pltpu.VMEM((2, 128, 256), BF16),
            pltpu.VMEM((NZ, 2, 2, 128, 512), BF16),
            pltpu.VMEM((NZ, 2, 2, 128, 256), BF16),
            pltpu.VMEM((2, BLOCK, 512), F32),
            pltpu.VMEM((2, BLOCK, 256), F32),
            pltpu.VMEM((7, 2, 2, BLOCK, HEAD_DIM), BF16),
            pltpu.VMEM((2, 2, BLOCK, HEAD_DIM), BF16),
            pltpu.VMEM((2, 2, BLOCK, HEAD_DIM), F32),
            pltpu.VMEM((2, 2, BLOCK, 128), F32),
            pltpu.VMEM((2, 2, BLOCK, 128), F32),
            pltpu.VMEM((2, BLOCK, 256), BF16),
            pltpu.VMEM((BLOCK, 256), BF16),
            dma((2,)), dma((2,)),
            dma((8,)), dma((8,)),
            dma((2, 2, 20)), dma((2, 2, 20)),
            dma((2,)), dma((2,)),
            dma((2, 8)), dma((2, 8)),
            dma((2, 8)), dma((2, 8)),
            dma((5, 2)), dma((5, 2)),
            dma((1,)), dma((1,)),
        ],
        compiler_params=pltpu.CompilerParams(
            collective_id=0, has_side_effects=True, vmem_limit_bytes=56 * 1024 * 1024
        ),
    )(
        pick.astype(jnp.int32), slot.astype(jnp.int32), bias.reshape(-1), latents,
        jnp.broadcast_to(norm_gain[None, :], (16, SLICE)), w_qkv.reshape(128, 4 * 384), cosine, sine,
    )
    return jnp.transpose(out.reshape(2, BLOCK, 2, HEAD_DIM), (1, 0, 2, 3)).reshape(BLOCK, 4, HEAD_DIM)


def solution(mesh):
    placed = (P("ctx", "head"), P("head"), P("ctx", "head", None), P(), P())
    return jax.shard_map(
        per_device, mesh=mesh, in_specs=placed, out_specs=P("ctx", "head", None), check_vma=False
    )
```

```python
import math

import jax
import jax.numpy as jnp
from jax import lax
from jax.experimental import pallas as pl
from jax.experimental.pallas import tpu as pltpu
from jax.sharding import PartitionSpec as P

HEAD_DIM = 128
UNITS_DEV = 16
STEPS = 4
EPS = 1e-05
ROPE_BASE = 50000000.0

BLOCK = 512
UNIT = BLOCK // UNITS_DEV
SLICE = 512
HALF = UNIT // 2
ROWS = BLOCK // 2
NZ, NY, NX = 8, 4, 4
CYCLE = 32
WIDTH = 4096
MESH = pl.DeviceIdType.MESH
F32, BF16 = jnp.float32, jnp.bfloat16
DELTA = (0, -1, 1, 2)
CHUNKS = ((0, 0, 512), (1, 0, 512))
SHARES = ((0, 96), (96, 160))
BASE2 = math.log2(math.e) * HEAD_DIM**-0.5


def kernel(*refs):
    unit_ref, first_ref, lat_ref, gain_ref, w_ref, far_ref, near_ref, out_ref = refs[:8]
    refs = refs[8:]
    n = len(CHUNKS)
    sbuf, rbuf, refs = refs[:n], refs[n : 2 * n], refs[2 * n :]
    (pick, ssrc, ssend, srecv, xg, own_sum, all_sums, wstage_kv, wstage_q, wkv, wq, acc_kv, acc_q, kvb, qb,
     unseen, cosine, sine, att, mrow, lrow, obuf, oswap,
     a_send, a_recv, s_send, s_recv, g_send, g_recv, x_send, x_recv, y_send, y_recv, z_send, z_recv,
     c_send, c_recv, h_send, h_recv, o_send, o_recv) = refs
    ctx, head = lax.axis_index("ctx"), lax.axis_index("head")
    z, yh, c = ctx // 4, (ctx // 2) % 2, ctx % 2
    yl, x = head // 4, head % 4
    y = yh * 2 + yl

    def place(at_x, at_y):
        at_x, at_y = lax.rem(at_x + 4, 4), lax.rem(at_y + 4, 4)
        return at_y // 2, lax.rem(at_y, 2) * 4 + at_x

    def device(at_x, at_y, at_z, at_c):
        row, column = place(at_x, at_y)
        return (lax.rem(at_z + NZ, NZ) * 4 + row * 2 + at_c, column)

    right, left = device(x + 1, y, z, c), device(x - 1, y, z, c)
    up, down = device(x, y + 1, z, c), device(x, y - 1, z, c)
    above, below = device(x, y, z + 1, c), device(x, y, z - 1, c)
    sibling = device(x, y, z, 1 - c)
    partner = device(x, y + 2, z, c)

    def copy(src, dst, send, recv, to):
        return pltpu.make_async_remote_copy(
            src_ref=src, dst_ref=dst, send_sem=send, recv_sem=recv, device_id=to, device_id_type=MESH
        )

    barrier = pltpu.get_barrier_semaphore()

    @pl.loop(1, CYCLE)
    def _(step):
        pl.semaphore_signal(barrier, inc=1, device_id=(lax.rem(ctx + step, CYCLE), head), device_id_type=MESH)

    @pl.loop(1, 8)
    def _(step):
        pl.semaphore_signal(barrier, inc=1, device_id=(ctx, lax.rem(head + step, 8)), device_id_type=MESH)

    for to in (up, down):
        pl.semaphore_signal(barrier, inc=1, device_id=to, device_id_type=MESH)

    @pl.loop(0, CYCLE)
    def _(step):
        start = lax.rem(ctx + step, CYCLE) * UNITS_DEV
        chosen = jnp.int32(0)
        for at in range(UNITS_DEV):
            value = unit_ref[start + at]
            chosen = chosen + jnp.where(lax.shift_right_logical(value, 4) == ctx, value & 15, 0)
        pick[step] = chosen

    def fill(chunk):
        part, low, high = CHUNKS[chunk]

        @pl.loop(0, CYCLE)
        def _(step):
            sbuf[chunk][step] = lat_ref[pick[step], part * HALF : (part + 1) * HALF, low:high]

    fill(0)

    eye = lax.broadcasted_iota(jnp.int32, (128, 128), 0) == lax.broadcasted_iota(jnp.int32, (128, 128), 1)
    for at in range(4):
        rows = lat_ref[at * 4 : (at + 1) * 4].astype(F32).reshape(128, SLICE)
        sums = jnp.sum(rows * rows, -1, keepdims=True)
        own_sum[:, at * 128 : (at + 1) * 128] = jnp.sum(jnp.where(eye, sums, 0.0), 0, keepdims=True)
    all_sums[head] = own_sum[...]

    pl.semaphore_wait(barrier, CYCLE - 1 + 7 + 2)

    def sum_copy(step):
        return copy(
            own_sum, all_sums.at[head], g_send.at[step], g_recv.at[head], (ctx, lax.rem(head + step, 8))
        )

    def sum_arrival(step):
        origin = lax.rem(head + step, 8)
        return copy(own_sum, all_sums.at[origin], g_send.at[step], g_recv.at[origin], (ctx, origin))

    @pl.loop(1, 8)
    def _(step):
        sum_copy(step).start()

    def unit_copy(chunk, step):
        return copy(
            sbuf[chunk].at[step], rbuf[chunk].at[step], a_send.at[chunk], a_recv.at[chunk],
            (lax.rem(ctx + step, CYCLE), head),
        )

    def units(chunk):
        others = pl.ds(1, CYCLE - 1)
        return copy(
            sbuf[chunk].at[others], rbuf[chunk].at[others], a_send.at[chunk], a_recv.at[chunk], sibling
        )

    def scale_copy(step):
        return copy(ssend.at[step], srecv.at[step], s_send.at[0], s_recv.at[0], (lax.rem(ctx + step, CYCLE), head))

    def scales():
        others = pl.ds(1, CYCLE - 1)
        return copy(ssend.at[others], srecv.at[others], s_send.at[0], s_recv.at[0], sibling)

    def to_all(one):
        @pl.loop(1, CYCLE // 2)
        def _(step):
            one(step).start()
            one(CYCLE - step).start()

        one(CYCLE // 2).start()

    def send_units(chunk):
        to_all(lambda step: unit_copy(chunk, step))

    send_units(0)

    for at in range(4):
        pair, side = at // 2, at % 2
        start = at * 384
        wstage_q[pair, :, side * 128 : (side + 1) * 128] = w_ref[:, start : start + 128]
        wstage_kv[pair, :, side * 128 : (side + 1) * 128] = w_ref[:, start + 128 : start + 256]
        wstage_kv[pair, :, 256 + side * 128 : 256 + (side + 1) * 128] = w_ref[:, start + 256 : start + 384]
    stages, weights = (wstage_kv, wstage_q), (wkv, wq)

    def swap_copy(kind, row):
        return copy(
            stages[kind].at[1 - row], weights[kind].at[z, c, row], y_send.at[kind], y_recv.at[kind], partner
        )

    for kind in range(2):
        swap_copy(kind, yh).start()
        weights[kind][z, c, yh] = stages[kind][yh]

    for chunk in range(1, n):
        fill(chunk)

    for part in range(2):
        row_at = lax.broadcasted_iota(jnp.int32, (ROWS, BLOCK), 0)
        key_at = lax.broadcasted_iota(jnp.int32, (ROWS, BLOCK), 1)
        row_pos = (row_at & ~15) * 2 + part * HALF + (row_at & 15)
        key_part = jnp.where(key_at >= ROWS, 1, 0)
        key_low = key_at - key_part * ROWS
        key_pos = (key_low & ~15) * 2 + key_part * HALF + (key_low & 15)
        unseen[part] = jnp.where(row_pos >= key_pos, 0.0, -1e30).astype(F32)

    for row in range(2):

        @pl.loop(0, 32)
        def _(at, row=row):
            far_cos, far_sin = far_ref[0, row, at], far_ref[1, row, at]
            near_cos, near_sin = near_ref[0], near_ref[1]
            to = lax.rem(at, 2) * 16 + at // 2
            cosine[row, to] = far_cos * near_cos - far_sin * near_sin
            sine[row, to] = far_sin * near_cos + far_cos * near_sin

    @pl.loop(1, 8)
    def _(step):
        sum_arrival(step).wait_recv()

    inverse = lax.rsqrt(jnp.sum(all_sums[...], 0) / WIDTH + EPS)
    for at in range(4):
        ssrc[at] = inverse[:, at * 128 : (at + 1) * 128]

    @pl.loop(0, CYCLE)
    def _(step):
        ssend[step] = ssrc[lax.shift_right_logical(pick[step], 2)]

    to_all(scale_copy)

    def x_region(chunk, half, first, second, quarter=None):
        part, low, high = CHUNKS[chunk]
        at = place(first, second) if half == 0 else place(second, first)
        start, size = SHARES[half]
        if quarter is not None:
            size = size // 2
            start += quarter * size
        return xg.at[part, at[0], at[1], pl.ds(start, size), pl.ds(low, high - low)]

    me_at = ((x, y), (y, x))
    ways = (((right, left), (up, down)), ((up, down), (right, left)))

    def x_copy(chunk, half, stage, s, way, receive=False):
        first, second = me_at[half]
        back = (-1 if way == 0 else 1) * (1 if receive else 0)
        on = -1 if way == 0 else 1
        if stage == 0:
            region, axis = x_region(chunk, half, first + back, second), 0
        elif stage == 1:
            region, axis = x_region(chunk, half, first + on + back, second, way), 0
        elif stage == 2:
            region, axis = x_region(chunk, half, first + DELTA[s], second + back), 1
        else:
            region, axis = x_region(chunk, half, first + DELTA[s], second + on + back, way), 1
        sem = (0, 2, 4, 12)[stage] + s * 2 + way
        return copy(
            region, region, x_send.at[chunk, half, sem], x_recv.at[chunk, half, sem], ways[half][axis][way]
        )

    def x_start(chunk, stage, s, way):
        for half in range(2):
            x_copy(chunk, half, stage, s, way).start()

    def x_wait(chunk, half, stage, s, way):
        x_copy(chunk, half, stage, s, way, receive=True).wait_recv()

    gain = gain_ref[...].astype(F32)
    lanes = lax.broadcasted_iota(jnp.int32, (HALF, 128), 1) - lax.broadcasted_iota(jnp.int32, (HALF, 128), 0)

    def arrange(chunk):
        part, low, high = CHUNKS[chunk]
        rbuf[chunk][0] = sbuf[chunk][0]
        units(chunk).wait_recv()
        for at in range(UNITS_DEV):
            source = unit_ref[ctx * UNITS_DEV + at]
            slot = (ctx - lax.shift_right_logical(source, 4)) & (CYCLE - 1)
            across = jnp.broadcast_to(srecv[slot], (HALF, 128))
            lane = (source & 3) * UNIT + part * HALF
            scale = jnp.sum(jnp.where(lanes == lane, across, 0.0), -1, keepdims=True)
            rows = rbuf[chunk][slot].astype(F32) * scale * gain[:, low:high]
            xg[part, yh, head, at * HALF : (at + 1) * HALF, low:high] = rows.astype(BF16)

    def begin(chunk):
        for stage in (0, 2):
            for way in range(2):
                x_start(chunk, stage, 0, way)

    def first_axis(chunk):
        for way in range(2):
            for half in range(2):
                x_wait(chunk, half, 0, 0, way)
                x_copy(chunk, half, 1, 0, way).start()
        for s in (1, 2):
            for way in range(2):
                x_start(chunk, 2, s, way)

    def first_axis_end(chunk):
        for half in range(2):
            for way in range(2):
                x_wait(chunk, half, 1, 0, way)
        for way in range(2):
            x_start(chunk, 2, 3, way)

    def second_axis(chunk, s):
        for way in range(2):
            for half in range(2):
                x_wait(chunk, half, 2, s, way)
                x_copy(chunk, half, 3, s, way).start()

    def second_axis_end(chunk):
        for s in range(4):
            for half in range(2):
                for way in range(2):
                    x_wait(chunk, half, 3, s, way)

    def w_copy(kind, hop, way, receive=False):
        on = (-1 if way == 0 else 1) * (hop if receive else hop - 1)
        region = weights[kind].at[lax.rem(z + on + NZ, NZ), c]
        sem = (hop - 1) * 2 + way
        return copy(region, region, z_send.at[kind, sem], z_recv.at[kind, sem], (above, below)[way])

    def w_share(kind, at, receive=False):
        region = weights[kind].at[lax.rem(z + at, NZ), 1 - c if receive else c]
        return copy(region, region, c_send.at[kind, at], c_recv.at[kind, at], sibling)

    def w_hop(kind, hop):
        if hop == 1:
            swap_copy(kind, 1 - yh).wait_recv()
            w_share(kind, 0).start()
        for way in range(2):
            last = 3 + way
            if 1 < hop <= last + 1:
                w_copy(kind, hop - 1, way, receive=True).wait_recv()
            if hop <= last:
                w_copy(kind, hop, way).start()
            if 1 < hop <= last + 1:
                w_share(kind, (NZ - (hop - 1)) if way == 0 else hop - 1).start()

    def project(kind, part):
        acc = (acc_kv, acc_q)[kind]

        def one(k):
            w_rows = jnp.concatenate([weights[kind][k, core, row] for row in range(2) for core in range(2)], 0)
            rows = xg[part, :, k].reshape(2 * ROWS, SLICE)
            return jnp.dot(rows, w_rows, preferred_element_type=F32)

        acc[...] = one(0)

        @pl.loop(1, 8)
        def _(k):
            acc[...] += one(k)

    def turn(value, part, row):
        places = slice(part * 16, (part + 1) * 16)
        cos_at, sin_at = cosine[row, places].reshape(ROWS, 128), sine[row, places].reshape(ROWS, 128)
        return value * cos_at + pltpu.roll(value, HEAD_DIM // 2, 1) * sin_at

    def halo(which, part, receive=False):
        if which == 0:
            src, dst, to = 5 + c, 1 + c, above
        elif which == 1:
            src, dst, to = 1 + c, 2 - c if receive else 1 + c, sibling
        elif which == 2:
            src, dst, to = 3 + c, 4 - c if receive else 3 + c, sibling
        elif which == 3:
            src, dst, to = 5, 5, sibling
        else:
            src, dst, to = 4, 0, device(x, y, z + 1, 0)
        return copy(
            kvb.at[src, part], kvb.at[dst, part], h_send.at[which, part], h_recv.at[which, part], to
        )

    def keys_values(part):
        project(0, part)
        for row in (1, 0):
            at = 2 * row + 3 + c
            rows = slice(row * ROWS, (row + 1) * ROWS)
            for side in range(2):
                keys = acc_kv[rows, side * 128 : (side + 1) * 128]
                vals = acc_kv[rows, 256 + side * 128 : 256 + (side + 1) * 128]
                kvb[at, part, side, 0] = turn(keys, part, row).astype(BF16)
                kvb[at, part, side, 1] = vals.astype(BF16)
            if row == 1:
                halo(0, part).start()

                @pl.when(c == 0)
                def _():
                    halo(3, part).start()

            else:

                @pl.when(c == 1)
                def _():
                    halo(4, part).start()

                halo(2, part).start()

    def queries(part):
        project(1, part)
        for row in range(2):
            rows = slice(row * ROWS, (row + 1) * ROWS)
            for side in range(2):
                query = acc_q[rows, side * 128 : (side + 1) * 128]
                qb[row, side, part] = turn(query, part, row).astype(BF16)

    def pass_on(part):
        halo(0, part, receive=True).wait_recv()
        halo(1, part).start()

    def block_of(at, side, kind):
        return kvb[at, :, side, kind].reshape(BLOCK, HEAD_DIM)

    def attend(row, side, tile, lags, first):
        query = qb[row, side, tile]
        own = 2 * row + 3 + c
        block = (z * 4 + 2 * row + c + CYCLE - first_ref[0]) & (CYCLE - 1)
        pieces = []
        for lag in lags:
            keys = block_of(own - lag, side, 0)
            value = lax.dot_general(query, keys, (((1,), (1,)), ((), ())), preferred_element_type=F32) * BASE2
            if lag == 0:
                pieces.append((value + unseen[tile], 0.0, own))
            else:
                pieces.append((value, jnp.where(block >= lag, 0.0, -1e30).astype(F32), own - lag))
        peak = None
        for value, bias, _ in pieces:
            top = jnp.max(value, -1, keepdims=True) + bias
            peak = top if peak is None else jnp.maximum(peak, top)
        if not first:
            before = mrow[row, side, tile, :, :1]
            peak = jnp.maximum(peak, before)
        total, summed = None, None
        for value, bias, at in pieces:
            weight = jnp.exp2(value - (peak - bias))
            part_total = jnp.sum(weight, -1, keepdims=True)
            part_sum = jnp.dot(weight.astype(BF16), block_of(at, side, 1), preferred_element_type=F32)
            total = part_total if total is None else total + part_total
            summed = part_sum if summed is None else summed + part_sum
        if not first:
            keep = jnp.exp2(before - peak)
            total = total + lrow[row, side, tile, :, :1] * keep
            summed = summed + att[row, side, tile] * keep
        return peak, total, summed

    def attend_some(row, side, lags, first=False):
        for tile in range(2):
            peak, total, summed = attend(row, side, tile, lags, first)
            mrow[row, side, tile] = jnp.broadcast_to(peak, (ROWS, 128))
            lrow[row, side, tile] = jnp.broadcast_to(total, (ROWS, 128))
            att[row, side, tile] = summed

    def attend_last(row, side, lags):
        for tile in range(2):
            _, total, summed = attend(row, side, tile, lags, False)
            obuf[row, side, :, tile] = (summed / total).astype(BF16).reshape(UNITS_DEV, HALF, HEAD_DIM)

    def out_copy(row, side):
        return copy(obuf.at[row, side], oswap.at[side], o_send.at[side], o_recv.at[side], partner)

    w_hop(0, 1)
    send_units(1)
    srecv[0] = ssend[0]
    scales().wait_recv()
    arrange(0)
    begin(0)
    w_hop(1, 1)
    first_axis(0)
    first_axis_end(0)
    w_hop(0, 2)
    second_axis(0, 0)
    second_axis(0, 1)
    w_hop(0, 3)
    second_axis(0, 2)
    second_axis(0, 3)
    arrange(1)
    begin(1)
    w_hop(1, 2)
    second_axis_end(0)
    w_hop(0, 4)
    first_axis(1)
    first_axis_end(1)
    w_hop(0, 5)
    second_axis(1, 0)
    w_hop(1, 3)
    for at in range(8):
        w_share(0, at, receive=True).wait_recv()
    keys_values(0)
    second_axis(1, 1)
    w_hop(1, 4)
    second_axis(1, 2)
    second_axis(1, 3)
    w_hop(1, 5)
    for at in range(8):
        w_share(1, at, receive=True).wait_recv()
    queries(0)
    pass_on(0)
    second_axis_end(1)
    keys_values(1)
    queries(1)
    for part in range(2):
        halo(2, part, receive=True).wait_recv()

        @pl.when(c == 1)
        def _(part=part):
            halo(3, part).wait_recv()

    for side in range(2):
        attend_some(1, side, (0, 1, 2), True)
        attend_some(0, side, (0,), True)
    pass_on(1)
    for part in range(2):
        halo(1, part, receive=True).wait_recv()
    for side in range(2):
        attend_last(1, side, (3,))

        @pl.when(yh == 0)
        def _(side=side):
            out_copy(1, side).start()

    for part in range(2):

        @pl.when(c == 0)
        def _(part=part):
            halo(4, part).wait_recv()

    for side in range(2):
        attend_last(0, side, (1, 2, 3))

        @pl.when(yh == 1)
        def _(side=side):
            out_copy(0, side).start()

    for side in range(2):
        out_ref[2 * yh + side] = obuf[yh, side].reshape(BLOCK, HEAD_DIM)
    for side in range(2):
        out_copy(yh, side).wait_recv()
        out_ref[2 - 2 * yh + side] = oswap[side].reshape(BLOCK, HEAD_DIM)

    @pl.loop(1, 8)
    def _(step):
        sum_copy(step).wait_send()

    scales().wait_send()
    for chunk in range(n):
        units(chunk).wait_send()
        for half in range(2):
            for way in range(2):
                for stage in range(4):
                    for s in range(4 if stage >= 2 else 1):
                        x_copy(chunk, half, stage, s, way).wait_send()
    for kind in range(2):
        swap_copy(kind, yh).wait_send()
        for way in range(2):
            for hop in range(1, 4 + way):
                w_copy(kind, hop, way).wait_send()
        for at in range(8):
            w_share(kind, at).wait_send()
    for part in range(2):
        for which in range(3):
            halo(which, part).wait_send()

        @pl.when(c == 0)
        def _(part=part):
            halo(3, part).wait_send()

        @pl.when(c == 1)
        def _(part=part):
            halo(4, part).wait_send()

    for side in range(2):
        out_copy(1 - yh, side).wait_send()


def per_device(latents, norm_gain, w_qkv, source_unit, first_block):
    own_index = lax.axis_index("ctx")
    own_blocks = own_index // 4 * 4 + own_index % 2 + jnp.array([0, 2], jnp.int32)
    block = (own_blocks - first_block[0]) % CYCLE
    half = HEAD_DIM // 2
    freq = jnp.exp(-math.log(ROPE_BASE) * jnp.arange(half, dtype=F32) * (2.0 / HEAD_DIM))
    freq = jnp.concatenate([freq, freq])
    sign = jnp.concatenate([-jnp.ones(half, F32), jnp.ones(half, F32)])
    starts = block[:, None] * BLOCK + 16 * jnp.arange(32, dtype=jnp.int32)[None, :]
    far = starts.astype(F32)[..., None] * freq
    near = jnp.arange(16, dtype=F32)[:, None] * freq
    far = jnp.stack([jnp.cos(far), jnp.sin(far) * sign]).reshape(2, 2, 32, 1, 128)
    near = jnp.stack([jnp.cos(near), jnp.sin(near) * sign])
    smem, vmem = pl.BlockSpec(memory_space=pltpu.SMEM), pl.BlockSpec(memory_space=pltpu.VMEM)
    dma = pltpu.SemaphoreType.DMA
    unit_slots = [pltpu.VMEM((CYCLE, HALF, high - low), BF16) for _, low, high in CHUNKS]
    n = len(CHUNKS)
    out = pl.pallas_call(
        kernel,
        out_shape=jax.ShapeDtypeStruct((4, BLOCK, HEAD_DIM), BF16),
        in_specs=[smem] * 2 + [vmem] * 5,
        out_specs=vmem,
        scratch_shapes=unit_slots
        + unit_slots
        + [
            pltpu.SMEM((CYCLE,), jnp.int32),
            pltpu.VMEM((4, 1, 128), F32),
            pltpu.VMEM((CYCLE, 1, 128), F32),
            pltpu.VMEM((CYCLE, 1, 128), F32),
            pltpu.VMEM((2, 2, 8, ROWS, SLICE), BF16),
            pltpu.VMEM((1, BLOCK), F32),
            pltpu.VMEM((8, 1, BLOCK), F32),
            pltpu.VMEM((2, 128, 512), BF16),
            pltpu.VMEM((2, 128, 256), BF16),
            pltpu.VMEM((NZ, 2, 2, 128, 512), BF16),
            pltpu.VMEM((NZ, 2, 2, 128, 256), BF16),
            pltpu.VMEM((2 * ROWS, 512), F32),
            pltpu.VMEM((2 * ROWS, 256), F32),
            pltpu.VMEM((7, 2, 2, 2, ROWS, HEAD_DIM), BF16),
            pltpu.VMEM((2, 2, 2, ROWS, HEAD_DIM), BF16),
            pltpu.VMEM((2, ROWS, BLOCK), F32),
            pltpu.VMEM((2, 32, 16, 128), F32),
            pltpu.VMEM((2, 32, 16, 128), F32),
            pltpu.VMEM((2, 2, 2, ROWS, HEAD_DIM), F32),
            pltpu.VMEM((2, 2, 2, ROWS, 128), F32),
            pltpu.VMEM((2, 2, 2, ROWS, 128), F32),
            pltpu.VMEM((2, 2, UNITS_DEV, 2, HALF, HEAD_DIM), BF16),
            pltpu.VMEM((2, UNITS_DEV, 2, HALF, HEAD_DIM), BF16),
            dma((n,)), dma((n,)),
            dma((1,)), dma((1,)),
            dma((8,)), dma((8,)),
            dma((n, 2, 20)), dma((n, 2, 20)),
            dma((2,)), dma((2,)),
            dma((2, 8)), dma((2, 8)),
            dma((2, 8)), dma((2, 8)),
            dma((5, 2)), dma((5, 2)),
            dma((2,)), dma((2,)),
        ],
        compiler_params=pltpu.CompilerParams(
            collective_id=0, has_side_effects=True, vmem_limit_bytes=56 * 1024 * 1024
        ),
    )(
        source_unit, first_block, latents.reshape(UNITS_DEV, UNIT, SLICE), norm_gain.reshape(1, SLICE),
        w_qkv.reshape(128, 4 * 384), far, near,
    )
    return jnp.transpose(out, (1, 0, 2))


def solution(mesh):
    placed = (P("ctx", "head"), P("head"), P("ctx", "head", None), P(), P())
    return jax.shard_map(
        per_device, mesh=mesh, in_specs=placed, out_specs=P("ctx", "head", None), check_vma=False
    )
```

```python
import math

import jax
import jax.numpy as jnp
import numpy as np
from jax import lax
from jax.experimental import pallas as pl
from jax.experimental.pallas import tpu as pltpu
from jax.sharding import PartitionSpec as P

HEAD_DIM = 128
UNITS_DEV = 16
STEPS = 4
EPS = 1e-05
ROPE_BASE = 50000000.0

BLOCK = 512
UNIT = BLOCK // UNITS_DEV
SLICE = 512
HALF = UNIT // 2
ROWS = BLOCK // 2
NZ, NY, NX = 8, 4, 4
CYCLE = 32
WIDTH = 4096
MESH = pl.DeviceIdType.MESH
F32, BF16 = jnp.float32, jnp.bfloat16
DELTA = (0, -1, 1, 2)
CHUNKS = ((0, 0, 256), (0, 256, 512), (1, 0, 512))
SHARES = ((0, 128), (128, 128))
BASE2 = math.log2(math.e) * HEAD_DIM**-0.5


def kernel(*refs):
    unit_ref, first_ref, lat_ref, gain_ref, w_ref, base_ref, near_ref, out_ref = refs[:8]
    refs = refs[8:]
    n = len(CHUNKS)
    sbuf, rbuf, refs = refs[:n], refs[n : 2 * n], refs[2 * n :]
    (pick, ssrc, ssend, srecv, xg, own_sum, all_sums, wstage_kv, wstage_q, wkv, wq, acc_kv, acc_q, kvb, qb,
     unseen, cosine, sine, att, mrow, lrow, obuf, oswap,
     a_send, a_recv, s_send, s_recv, g_send, g_recv, x_send, x_recv, q_recv, y_send, y_recv, z_send, z_recv,
     c_send, c_recv, h_send, h_recv, o_send, o_recv) = refs
    ctx, head = lax.axis_index("ctx"), lax.axis_index("head")
    z, yh, c = ctx // 4, (ctx // 2) % 2, ctx % 2
    yl, x = head // 4, head % 4
    y = yh * 2 + yl

    def place(at_x, at_y):
        return lax.rem(at_y + 4, 4) * 4 + lax.rem(at_x + 4, 4)

    def device(at_x, at_y, at_z, at_c):
        at = place(at_x, at_y)
        return (lax.rem(at_z + NZ, NZ) * 4 + at // 8 * 2 + at_c, lax.rem(at, 8))

    right, left = device(x + 1, y, z, c), device(x - 1, y, z, c)
    up, down = device(x, y + 1, z, c), device(x, y - 1, z, c)
    above, below = device(x, y, z + 1, c), device(x, y, z - 1, c)
    sibling = device(x, y, z, 1 - c)
    partner = device(x, y + 2, z, c)

    def copy(src, dst, send, recv, to):
        return pltpu.make_async_remote_copy(
            src_ref=src, dst_ref=dst, send_sem=send, recv_sem=recv, device_id=to, device_id_type=MESH
        )

    barrier = pltpu.get_barrier_semaphore()

    @pl.loop(1, CYCLE)
    def _(step):
        pl.semaphore_signal(barrier, inc=1, device_id=(lax.rem(ctx + step, CYCLE), head), device_id_type=MESH)

    @pl.loop(1, 8)
    def _(step):
        pl.semaphore_signal(barrier, inc=1, device_id=(ctx, lax.rem(head + step, 8)), device_id_type=MESH)

    for to in (up, down):
        pl.semaphore_signal(barrier, inc=1, device_id=to, device_id_type=MESH)

    @pl.loop(0, CYCLE)
    def _(step):
        start = lax.rem(ctx + step, CYCLE) * UNITS_DEV
        chosen = jnp.int32(0)
        for at in range(UNITS_DEV):
            value = unit_ref[start + at]
            chosen = chosen + jnp.where(lax.shift_right_logical(value, 4) == ctx, value & 15, 0)
        pick[step] = chosen

    def fill(chunk):
        part, low, high = CHUNKS[chunk]

        @pl.loop(0, CYCLE)
        def _(step):
            sbuf[chunk][step] = lat_ref[pick[step], part * HALF : (part + 1) * HALF, low:high]

    fill(0)

    eye = lax.broadcasted_iota(jnp.int32, (128, 128), 0) == lax.broadcasted_iota(jnp.int32, (128, 128), 1)
    for at in range(4):
        rows = lat_ref[at * 4 : (at + 1) * 4].astype(F32).reshape(128, SLICE)
        sums = jnp.sum(rows * rows, -1, keepdims=True)
        own_sum[:, at * 128 : (at + 1) * 128] = jnp.sum(jnp.where(eye, sums, 0.0), 0, keepdims=True)
    all_sums[head] = own_sum[...]

    pl.semaphore_wait(barrier, CYCLE - 1 + 7 + 2)

    def sum_copy(step):
        return copy(
            own_sum, all_sums.at[head], g_send.at[0], g_recv.at[0], (ctx, lax.rem(head + step, 8))
        )

    def sums_of_others():
        others = all_sums.at[pl.ds(0, 7)]
        return copy(others, others, g_send.at[0], g_recv.at[0], sibling)

    @pl.loop(1, 8)
    def _(step):
        sum_copy(step).start()

    def unit_copy(chunk, step):
        return copy(
            sbuf[chunk].at[step], rbuf[chunk].at[step], a_send.at[chunk], a_recv.at[chunk],
            (lax.rem(ctx + step, CYCLE), head),
        )

    def units(chunk):
        others = pl.ds(1, CYCLE - 1)
        return copy(
            sbuf[chunk].at[others], rbuf[chunk].at[others], a_send.at[chunk], a_recv.at[chunk], sibling
        )

    def scale_copy(step):
        return copy(ssend.at[step], srecv.at[step], s_send.at[0], s_recv.at[0], (lax.rem(ctx + step, CYCLE), head))

    def scales():
        others = pl.ds(1, CYCLE - 1)
        return copy(ssend.at[others], srecv.at[others], s_send.at[0], s_recv.at[0], sibling)

    def to_all(one):
        @pl.loop(1, CYCLE // 2)
        def _(step):
            one(step).start()
            one(CYCLE - step).start()

        one(CYCLE // 2).start()

    def send_units(chunk):
        to_all(lambda step: unit_copy(chunk, step))

    send_units(0)

    for at in range(4):
        pair, side = at // 2, at % 2
        wstage_q[pair, :, side * 128 : (side + 1) * 128] = w_ref[:, at, :128]
        wstage_kv[pair, :, side * 128 : (side + 1) * 128] = w_ref[:, at, 128:256]
        wstage_kv[pair, :, 256 + side * 128 : 256 + (side + 1) * 128] = w_ref[:, at, 256:]
    stages, weights = (wstage_kv, wstage_q), (wkv, wq)

    def swap_copy(kind, row):
        return copy(
            stages[kind].at[1 - row], weights[kind].at[z, c, row], y_send.at[kind], y_recv.at[kind], partner
        )

    for kind in range(2):
        swap_copy(kind, yh).start()
        weights[kind][z, c, yh] = stages[kind][yh]

    for chunk in range(1, n):
        fill(chunk)

    for part in range(2):
        row_at = lax.broadcasted_iota(jnp.int32, (ROWS, BLOCK), 0)
        key_at = lax.broadcasted_iota(jnp.int32, (ROWS, BLOCK), 1)
        row_pos = (row_at & ~15) * 2 + part * HALF + (row_at & 15)
        key_part = jnp.where(key_at >= ROWS, 1, 0)
        key_low = key_at - key_part * ROWS
        key_pos = (key_low & ~15) * 2 + key_part * HALF + (key_low & 15)
        unseen[part] = jnp.where(row_pos >= key_pos, 0.0, -1e30).astype(F32)

    for row in range(2):
        block = (z * 4 + 2 * row + c + CYCLE - first_ref[0]) & (CYCLE - 1)
        base_cos, base_sin = base_ref[0, block], base_ref[1, block]

        @pl.loop(0, 32)
        def _(at, row=row, base_cos=base_cos, base_sin=base_sin):
            step_cos, step_sin = base_ref[0, CYCLE + at], base_ref[1, CYCLE + at]
            far_cos = base_cos * step_cos - base_sin * step_sin
            far_sin = base_sin * step_cos + base_cos * step_sin
            near_cos, near_sin = near_ref[0], near_ref[1]
            to = lax.rem(at, 2) * 16 + at // 2
            cosine[row, to] = far_cos * near_cos - far_sin * near_sin
            sine[row, to] = far_sin * near_cos + far_cos * near_sin

    sums_of_others().wait_recv()

    inverse = lax.rsqrt(jnp.sum(all_sums[...], 0) / WIDTH + EPS)
    for at in range(4):
        ssrc[at] = inverse[:, at * 128 : (at + 1) * 128]

    @pl.loop(0, CYCLE)
    def _(step):
        ssend[step] = ssrc[lax.shift_right_logical(pick[step], 2)]

    to_all(scale_copy)

    def x_region(chunk, half, first, second, quarter=None):
        part, low, high = CHUNKS[chunk]
        at = place(first, second) if half == 0 else place(second, first)
        start, size = SHARES[half]
        if quarter is not None:
            size = size // 2
            start += quarter * size
        return xg.at[part, at, pl.ds(start, size), pl.ds(low, high - low)]

    me_at = ((x, y), (y, x))
    ways = (((right, left), (up, down)), ((up, down), (right, left)))

    def x_copy(chunk, half, stage, s, way, receive=False):
        first, second = me_at[half]
        back = (-1 if way == 0 else 1) * (1 if receive else 0)
        on = -1 if way == 0 else 1
        if stage == 0:
            region, axis = x_region(chunk, half, first + back, second), 0
        elif stage == 1:
            region, axis = x_region(chunk, half, first + on + back, second, way), 0
        elif stage == 2:
            region, axis = x_region(chunk, half, first + DELTA[s], second + back), 1
        else:
            region, axis = x_region(chunk, half, first + DELTA[s], second + on + back, way), 1
        arrived = q_recv.at[chunk] if stage == 3 else x_recv.at[chunk, half, (0, 2, 4)[stage] + s * 2 + way]
        return copy(region, region, x_send.at[chunk], arrived, ways[half][axis][way])

    def x_several(chunk, pieces):
        part, low, high = CHUNKS[chunk]
        region = xg.at[part, pl.ds(0, pieces), :, pl.ds(low, high - low)]
        return copy(region, region, x_send.at[chunk], q_recv.at[chunk], right)

    def x_start(chunk, stage, s, way):
        for half in range(2):
            x_copy(chunk, half, stage, s, way).start()

    def x_wait(chunk, half, stage, s, way):
        x_copy(chunk, half, stage, s, way, receive=True).wait_recv()

    gain = gain_ref[...].astype(F32).reshape(1, SLICE)
    lanes = lax.broadcasted_iota(jnp.int32, (HALF, 128), 1) - lax.broadcasted_iota(jnp.int32, (HALF, 128), 0)

    def arrange(chunk):
        part, low, high = CHUNKS[chunk]
        rbuf[chunk][0] = sbuf[chunk][0]
        units(chunk).wait_recv()
        for at in range(UNITS_DEV):
            source = unit_ref[ctx * UNITS_DEV + at]
            slot = (ctx - lax.shift_right_logical(source, 4)) & (CYCLE - 1)
            across = jnp.broadcast_to(srecv[slot], (HALF, 128))
            lane = (source & 3) * UNIT + part * HALF
            scale = jnp.sum(jnp.where(lanes == lane, across, 0.0), -1, keepdims=True)
            rows = rbuf[chunk][slot].astype(F32) * scale * gain[:, low:high]
            xg[part, yh * 8 + head, at * HALF : (at + 1) * HALF, low:high] = rows.astype(BF16)

    def begin(chunk):
        for stage in (0, 2):
            for way in range(2):
                x_start(chunk, stage, 0, way)

    def first_axis(chunk):
        for way in range(2):
            for half in range(2):
                x_wait(chunk, half, 0, 0, way)
                x_copy(chunk, half, 1, 0, way).start()
        for s in (1, 2):
            for way in range(2):
                x_start(chunk, 2, s, way)

    def first_axis_end(chunk):
        for half in range(2):
            for way in range(2):
                x_wait(chunk, half, 1, 0, way)
        for way in range(2):
            x_start(chunk, 2, 3, way)

    def second_axis(chunk, s):
        for way in range(2):
            for half in range(2):
                x_wait(chunk, half, 2, s, way)
                x_copy(chunk, half, 3, s, way).start()

    def second_axis_end(chunk):
        x_several(chunk, 4).wait_recv()

    def w_copy(kind, hop, way, receive=False):
        on = (-1 if way == 0 else 1) * (hop if receive else hop - 1)
        region = weights[kind].at[lax.rem(z + on + NZ, NZ), c]
        sem = (hop - 1) * 2 + way
        return copy(region, region, z_send.at[kind], z_recv.at[kind, sem], (above, below)[way])

    def w_several(kind, pieces, send, recv):
        region = weights[kind].at[pl.ds(0, pieces), 0]
        return copy(region, region, send.at[kind], recv.at[kind], sibling)

    def w_share(kind, at):
        region = weights[kind].at[lax.rem(z + at, NZ), c]
        return copy(region, region, c_send.at[kind], c_recv.at[kind], sibling)

    def w_hop(kind, hop):
        if hop == 1:
            swap_copy(kind, 1 - yh).wait_recv()
            w_share(kind, 0).start()
        for way in range(2):
            last = 3 + way
            if 1 < hop <= last + 1:
                w_copy(kind, hop - 1, way, receive=True).wait_recv()
            if hop <= last:
                w_copy(kind, hop, way).start()
            if 1 < hop <= last + 1:
                w_share(kind, (NZ - (hop - 1)) if way == 0 else hop - 1).start()

    def project(kind, part):
        acc = (acc_kv, acc_q)[kind]

        def one(k):
            w_rows = jnp.concatenate([weights[kind][k, core, row] for row in range(2) for core in range(2)], 0)
            rows = jnp.concatenate([xg[part, k], xg[part, 8 + k]], 0)
            return jnp.dot(rows, w_rows, preferred_element_type=F32)

        acc[...] = one(0)

        @pl.loop(1, 8)
        def _(k):
            acc[...] += one(k)

    def turn(value, part, row):
        places = slice(part * 16, (part + 1) * 16)
        cos_at, sin_at = cosine[row, places].reshape(ROWS, 128), sine[row, places].reshape(ROWS, 128)
        return value * cos_at + pltpu.roll(value, HEAD_DIM // 2, 1) * sin_at

    def halo(which, part, receive=False):
        if which == 0:
            src, dst, to = 5 + c, 1 + c, above
        elif which == 1:
            src, dst, to = 1 + c, 2 - c if receive else 1 + c, sibling
        elif which == 2:
            src, dst, to = 3 + c, 4 - c if receive else 3 + c, sibling
        elif which == 3:
            src, dst, to = 5, 5, sibling
        else:
            src, dst, to = 4, 0, device(x, y, z + 1, 0)
        return copy(
            kvb.at[src, part], kvb.at[dst, part], h_send.at[which, part], h_recv.at[which, part], to
        )

    def keys_values(part):
        project(0, part)
        for row in (1, 0):
            at = 2 * row + 3 + c
            rows = slice(row * ROWS, (row + 1) * ROWS)
            for side in range(2):
                keys = acc_kv[rows, side * 128 : (side + 1) * 128]
                vals = acc_kv[rows, 256 + side * 128 : 256 + (side + 1) * 128]
                kvb[at, part, side, 0] = turn(keys, part, row).astype(BF16)
                kvb[at, part, side, 1] = vals.astype(BF16)
            if row == 1:
                halo(0, part).start()

                @pl.when(c == 0)
                def _():
                    halo(3, part).start()

            else:

                @pl.when(c == 1)
                def _():
                    halo(4, part).start()

                halo(2, part).start()

    def queries(part):
        project(1, part)
        for row in range(2):
            rows = slice(row * ROWS, (row + 1) * ROWS)
            for side in range(2):
                query = acc_q[rows, side * 128 : (side + 1) * 128]
                qb[row, side, part] = turn(query, part, row).astype(BF16)

    def pass_on(part):
        halo(0, part, receive=True).wait_recv()
        halo(1, part).start()

    def block_of(at, side, kind):
        return kvb[at, :, side, kind].reshape(BLOCK, HEAD_DIM)

    def attend(row, side, tile, lags, first):
        query = qb[row, side, tile]
        own = 2 * row + 3 + c
        block = (z * 4 + 2 * row + c + CYCLE - first_ref[0]) & (CYCLE - 1)
        pieces = []
        for lag in lags:
            keys = block_of(own - lag, side, 0)
            value = lax.dot_general(query, keys, (((1,), (1,)), ((), ())), preferred_element_type=F32) * BASE2
            if lag == 0:
                pieces.append((value + unseen[tile], 0.0, own))
            else:
                pieces.append((value, jnp.where(block >= lag, 0.0, -1e30).astype(F32), own - lag))
        peak = None
        for value, bias, _ in pieces:
            top = jnp.max(value, -1, keepdims=True) + bias
            peak = top if peak is None else jnp.maximum(peak, top)
        if not first:
            before = mrow[row, side, tile, :, :1]
            peak = jnp.maximum(peak, before)
        total, summed = None, None
        for value, bias, at in pieces:
            weight = jnp.exp2(value - (peak - bias))
            part_total = jnp.sum(weight, -1, keepdims=True)
            part_sum = jnp.dot(weight.astype(BF16), block_of(at, side, 1), preferred_element_type=F32)
            total = part_total if total is None else total + part_total
            summed = part_sum if summed is None else summed + part_sum
        if not first:
            keep = jnp.exp2(before - peak)
            total = total + lrow[row, side, tile, :, :1] * keep
            summed = summed + att[row, side, tile] * keep
        return peak, total, summed

    def attend_some(row, side, lags, first=False):
        for tile in range(2):
            peak, total, summed = attend(row, side, tile, lags, first)
            mrow[row, side, tile] = jnp.broadcast_to(peak, (ROWS, 128))
            lrow[row, side, tile] = jnp.broadcast_to(total, (ROWS, 128))
            att[row, side, tile] = summed

    def attend_last(row, side, lags):
        for tile in range(2):
            _, total, summed = attend(row, side, tile, lags, False)
            obuf[row, side, :, tile] = (summed / total).astype(BF16).reshape(UNITS_DEV, HALF, HEAD_DIM)

    def out_copy(row, side):
        return copy(obuf.at[row, side], oswap.at[side], o_send.at[side], o_recv.at[side], partner)

    srecv[0] = ssend[0]
    send_units(1)
    w_hop(0, 1)
    scales().wait_recv()
    arrange(0)
    begin(0)
    send_units(2)
    first_axis(0)
    w_hop(1, 1)
    arrange(1)
    begin(1)
    first_axis_end(0)
    w_hop(0, 2)
    second_axis(0, 0)
    first_axis(1)
    second_axis(0, 1)
    second_axis(0, 2)
    first_axis_end(1)
    second_axis(0, 3)
    w_hop(0, 3)
    second_axis(1, 0)
    second_axis(1, 1)
    second_axis_end(0)
    w_hop(1, 2)
    arrange(2)
    begin(2)
    second_axis(1, 2)
    second_axis(1, 3)
    w_hop(0, 4)
    second_axis_end(1)
    first_axis(2)
    first_axis_end(2)
    w_hop(0, 5)
    second_axis(2, 0)
    w_hop(1, 3)
    w_several(0, 8, c_send, c_recv).wait_recv()
    keys_values(0)
    second_axis(2, 1)
    w_hop(1, 4)
    second_axis(2, 2)
    second_axis(2, 3)
    w_hop(1, 5)
    w_several(1, 8, c_send, c_recv).wait_recv()
    queries(0)
    pass_on(0)
    second_axis_end(2)
    keys_values(1)
    queries(1)
    for part in range(2):
        halo(2, part, receive=True).wait_recv()

        @pl.when(c == 1)
        def _(part=part):
            halo(3, part).wait_recv()

    for side in range(2):
        attend_some(1, side, (0, 1, 2), True)
        attend_some(0, side, (0,), True)
    pass_on(1)
    for part in range(2):
        halo(1, part, receive=True).wait_recv()
    for side in range(2):
        attend_last(1, side, (3,))

        @pl.when(yh == 0)
        def _(side=side):
            out_copy(1, side).start()

    for part in range(2):

        @pl.when(c == 0)
        def _(part=part):
            halo(4, part).wait_recv()

    for side in range(2):
        attend_last(0, side, (1, 2, 3))

        @pl.when(yh == 1)
        def _(side=side):
            out_copy(0, side).start()

    for side in range(2):
        out_ref[2 * yh + side] = obuf[yh, side].reshape(BLOCK, HEAD_DIM)
    for side in range(2):
        out_copy(yh, side).wait_recv()
        out_ref[2 - 2 * yh + side] = oswap[side].reshape(BLOCK, HEAD_DIM)

    sums_of_others().wait_send()
    scales().wait_send()
    for chunk in range(n):
        units(chunk).wait_send()
        x_several(chunk, 15).wait_send()
    for kind in range(2):
        swap_copy(kind, yh).wait_send()
        w_several(kind, 7, z_send, c_recv).wait_send()
        w_several(kind, 8, c_send, c_recv).wait_send()
    for part in range(2):
        for which in range(3):
            halo(which, part).wait_send()

        @pl.when(c == 0)
        def _(part=part):
            halo(3, part).wait_send()

        @pl.when(c == 1)
        def _(part=part):
            halo(4, part).wait_send()

    for side in range(2):
        out_copy(1 - yh, side).wait_send()


def per_device(latents, norm_gain, w_qkv, source_unit, first_block):
    half = HEAD_DIM // 2
    freq = np.exp(-math.log(ROPE_BASE) * np.arange(half) * (2.0 / HEAD_DIM))
    freq = np.concatenate([freq, freq])
    sign = np.concatenate([-np.ones(half), np.ones(half)])

    def table(positions):
        angles = np.asarray(positions)[:, None] * freq
        return np.stack([np.cos(angles), np.sin(angles) * sign]).astype(np.float32)

    base = table(np.concatenate([np.arange(CYCLE) * BLOCK, np.arange(32) * 16]))[:, :, None]
    near = table(np.arange(16))
    smem, vmem = pl.BlockSpec(memory_space=pltpu.SMEM), pl.BlockSpec(memory_space=pltpu.VMEM)
    dma = pltpu.SemaphoreType.DMA
    unit_slots = [pltpu.VMEM((CYCLE, HALF, high - low), BF16) for _, low, high in CHUNKS]
    n = len(CHUNKS)
    out = pl.pallas_call(
        kernel,
        out_shape=jax.ShapeDtypeStruct((4, BLOCK, HEAD_DIM), BF16),
        in_specs=[smem] * 2 + [vmem] * 5,
        out_specs=vmem,
        scratch_shapes=unit_slots
        + unit_slots
        + [
            pltpu.SMEM((CYCLE,), jnp.int32),
            pltpu.VMEM((4, 1, 128), F32),
            pltpu.VMEM((CYCLE, 1, 128), F32),
            pltpu.VMEM((CYCLE, 1, 128), F32),
            pltpu.VMEM((2, 16, ROWS, SLICE), BF16),
            pltpu.VMEM((1, BLOCK), F32),
            pltpu.VMEM((8, 1, BLOCK), F32),
            pltpu.VMEM((2, 128, 512), BF16),
            pltpu.VMEM((2, 128, 256), BF16),
            pltpu.VMEM((NZ, 2, 2, 128, 512), BF16),
            pltpu.VMEM((NZ, 2, 2, 128, 256), BF16),
            pltpu.VMEM((2 * ROWS, 512), F32),
            pltpu.VMEM((2 * ROWS, 256), F32),
            pltpu.VMEM((7, 2, 2, 2, ROWS, HEAD_DIM), BF16),
            pltpu.VMEM((2, 2, 2, ROWS, HEAD_DIM), BF16),
            pltpu.VMEM((2, ROWS, BLOCK), F32),
            pltpu.VMEM((2, 32, 16, 128), F32),
            pltpu.VMEM((2, 32, 16, 128), F32),
            pltpu.VMEM((2, 2, 2, ROWS, HEAD_DIM), F32),
            pltpu.VMEM((2, 2, 2, ROWS, 128), F32),
            pltpu.VMEM((2, 2, 2, ROWS, 128), F32),
            pltpu.VMEM((2, 2, UNITS_DEV, 2, HALF, HEAD_DIM), BF16),
            pltpu.VMEM((2, UNITS_DEV, 2, HALF, HEAD_DIM), BF16),
            dma((n,)), dma((n,)),
            dma((1,)), dma((1,)),
            dma((1,)), dma((1,)),
            dma((n,)), dma((n, 2, 12)), dma((n,)),
            dma((2,)), dma((2,)),
            dma((2,)), dma((2, 8)),
            dma((2,)), dma((2,)),
            dma((5, 2)), dma((5, 2)),
            dma((2,)), dma((2,)),
        ],
        compiler_params=pltpu.CompilerParams(
            collective_id=0, has_side_effects=True, vmem_limit_bytes=56 * 1024 * 1024
        ),
    )(
        source_unit, first_block, latents.reshape(UNITS_DEV, UNIT, SLICE), norm_gain,
        w_qkv, base, near,
    )
    return jnp.transpose(out, (1, 0, 2))


def solution(mesh):
    placed = (P("ctx", "head"), P("head"), P("ctx", "head", None), P(), P())
    return jax.shard_map(
        per_device, mesh=mesh, in_specs=placed, out_specs=P("ctx", "head", None), check_vma=False
    )
```

```python
import math

import jax
import jax.numpy as jnp
import numpy as np
from jax import lax
from jax.experimental import pallas as pl
from jax.experimental.pallas import tpu as pltpu
from jax.sharding import PartitionSpec as P

HEAD_DIM = 128
UNITS_DEV = 16
STEPS = 4
EPS = 1e-05
ROPE_BASE = 50000000.0

BLOCK = 512
UNIT = BLOCK // UNITS_DEV
SLICE = 512
HALF = UNIT // 2
ROWS = BLOCK // 2
NZ, NY, NX = 8, 4, 4
CYCLE = 32
WIDTH = 4096
MESH = pl.DeviceIdType.MESH
F32, BF16 = jnp.float32, jnp.bfloat16
DELTA = (0, -1, 1, 2)
CHUNKS = ((0, 0, 256), (0, 256, 512), (1, 0, 512))
SHARES = ((0, 128), (128, 128))
BASE2 = math.log2(math.e) * HEAD_DIM**-0.5


def kernel(*refs):
    unit_ref, first_ref, lat_ref, gain_ref, w_ref, base_ref, near_ref, out_ref = refs[:8]
    refs = refs[8:]
    n = len(CHUNKS)
    sbuf, rbuf, refs = refs[:n], refs[n : 2 * n], refs[2 * n :]
    (pick, ssrc, ssend, srecv, xg, own_sum, all_sums, wstage_kv, wstage_q, wkv, wq, acc_kv, acc_q, kvb, qb,
     unseen, cosine, sine, att, mrow, lrow, obuf, oswap,
     a_send, a_recv, s_send, s_recv, g_send, g_recv, x_send, x_recv, q_recv, y_send, y_recv, z_send, z_recv,
     c_send, c_recv, h_send, h_recv, o_send, o_recv) = refs
    ctx, head = lax.axis_index("ctx"), lax.axis_index("head")
    z, yh, c = ctx // 4, (ctx // 2) % 2, ctx % 2
    yl, x = head // 4, head % 4
    y = yh * 2 + yl

    def place(at_x, at_y):
        return lax.rem(at_y + 4, 4) * 4 + lax.rem(at_x + 4, 4)

    def device(at_x, at_y, at_z, at_c):
        at = place(at_x, at_y)
        return (lax.rem(at_z + NZ, NZ) * 4 + at // 8 * 2 + at_c, lax.rem(at, 8))

    right, left = device(x + 1, y, z, c), device(x - 1, y, z, c)
    up, down = device(x, y + 1, z, c), device(x, y - 1, z, c)
    above, below = device(x, y, z + 1, c), device(x, y, z - 1, c)
    sibling = device(x, y, z, 1 - c)
    partner = device(x, y + 2, z, c)

    def copy(src, dst, send, recv, to):
        return pltpu.make_async_remote_copy(
            src_ref=src, dst_ref=dst, send_sem=send, recv_sem=recv, device_id=to, device_id_type=MESH
        )

    barrier = pltpu.get_barrier_semaphore()

    @pl.loop(1, CYCLE)
    def _(step):
        pl.semaphore_signal(barrier, inc=1, device_id=(lax.rem(ctx + step, CYCLE), head), device_id_type=MESH)

    @pl.loop(1, 8)
    def _(step):
        pl.semaphore_signal(barrier, inc=1, device_id=(ctx, lax.rem(head + step, 8)), device_id_type=MESH)

    for to in (up, down):
        pl.semaphore_signal(barrier, inc=1, device_id=to, device_id_type=MESH)

    @pl.loop(0, CYCLE)
    def _(step):
        start = lax.rem(ctx + step, CYCLE) * UNITS_DEV
        chosen = jnp.int32(0)
        for at in range(UNITS_DEV):
            value = unit_ref[start + at]
            chosen = chosen + jnp.where(lax.shift_right_logical(value, 4) == ctx, value & 15, 0)
        pick[step] = chosen

    def fill(chunk):
        part, low, high = CHUNKS[chunk]

        @pl.loop(0, CYCLE)
        def _(step):
            sbuf[chunk][step] = lat_ref[pick[step], part * HALF : (part + 1) * HALF, low:high]

    fill(0)

    eye = lax.broadcasted_iota(jnp.int32, (128, 128), 0) == lax.broadcasted_iota(jnp.int32, (128, 128), 1)
    for at in range(4):
        rows = lat_ref[at * 4 : (at + 1) * 4].astype(F32).reshape(128, SLICE)
        sums = jnp.sum(rows * rows, -1, keepdims=True)
        own_sum[:, at * 128 : (at + 1) * 128] = jnp.sum(jnp.where(eye, sums, 0.0), 0, keepdims=True)
    all_sums[head] = own_sum[...]

    pl.semaphore_wait(barrier, CYCLE - 1 + 7 + 2)

    def sum_copy(step):
        return copy(
            own_sum, all_sums.at[head], g_send.at[0], g_recv.at[0], (ctx, lax.rem(head + step, 8))
        )

    def sums_of_others():
        others = all_sums.at[pl.ds(0, 7)]
        return copy(others, others, g_send.at[0], g_recv.at[0], sibling)

    @pl.loop(1, 8)
    def _(step):
        sum_copy(step).start()

    def unit_copy(chunk, step):
        return copy(
            sbuf[chunk].at[step], rbuf[chunk].at[step], a_send.at[chunk], a_recv.at[chunk],
            (lax.rem(ctx + step, CYCLE), head),
        )

    def units(chunk):
        others = pl.ds(1, CYCLE - 1)
        return copy(
            sbuf[chunk].at[others], rbuf[chunk].at[others], a_send.at[chunk], a_recv.at[chunk], sibling
        )

    def scale_copy(step):
        return copy(ssend.at[step], srecv.at[step], s_send.at[0], s_recv.at[0], (lax.rem(ctx + step, CYCLE), head))

    def scales():
        others = pl.ds(1, CYCLE - 1)
        return copy(ssend.at[others], srecv.at[others], s_send.at[0], s_recv.at[0], sibling)

    def to_all(one):
        @pl.loop(1, CYCLE // 2)
        def _(step):
            one(step).start()
            one(CYCLE - step).start()

        one(CYCLE // 2).start()

    def send_units(chunk):
        to_all(lambda step: unit_copy(chunk, step))

    send_units(0)

    for at in range(4):
        pair, side = at // 2, at % 2
        wstage_q[pair, :, side * 128 : (side + 1) * 128] = w_ref[:, at, :128]
        wstage_kv[pair, :, side * 128 : (side + 1) * 128] = w_ref[:, at, 128:256]
        wstage_kv[pair, :, 256 + side * 128 : 256 + (side + 1) * 128] = w_ref[:, at, 256:]
    stages, weights = (wstage_kv, wstage_q), (wkv, wq)

    def swap_copy(kind, row):
        return copy(
            stages[kind].at[1 - row], weights[kind].at[z, c, row], y_send.at[kind], y_recv.at[kind], partner
        )

    for kind in range(2):
        swap_copy(kind, yh).start()
        weights[kind][z, c, yh] = stages[kind][yh]

    for chunk in range(1, n):
        fill(chunk)

    for part in range(2):
        row_at = lax.broadcasted_iota(jnp.int32, (ROWS, BLOCK), 0)
        key_at = lax.broadcasted_iota(jnp.int32, (ROWS, BLOCK), 1)
        row_pos = (row_at & ~15) * 2 + part * HALF + (row_at & 15)
        key_part = jnp.where(key_at >= ROWS, 1, 0)
        key_low = key_at - key_part * ROWS
        key_pos = (key_low & ~15) * 2 + key_part * HALF + (key_low & 15)
        unseen[part] = jnp.where(row_pos >= key_pos, 0.0, -1e30).astype(F32)

    for row in range(2):
        block = (z * 4 + 2 * row + c + CYCLE - first_ref[0]) & (CYCLE - 1)
        base_cos, base_sin = base_ref[0, block], base_ref[1, block]

        @pl.loop(0, 32)
        def _(at, row=row, base_cos=base_cos, base_sin=base_sin):
            step_cos, step_sin = base_ref[0, CYCLE + at], base_ref[1, CYCLE + at]
            far_cos = base_cos * step_cos - base_sin * step_sin
            far_sin = base_sin * step_cos + base_cos * step_sin
            near_cos, near_sin = near_ref[0], near_ref[1]
            to = lax.rem(at, 2) * 16 + at // 2
            cosine[row, to] = far_cos * near_cos - far_sin * near_sin
            sine[row, to] = far_sin * near_cos + far_cos * near_sin

    sums_of_others().wait_recv()

    inverse = lax.rsqrt(jnp.sum(all_sums[...], 0) / WIDTH + EPS)
    for at in range(4):
        ssrc[at] = inverse[:, at * 128 : (at + 1) * 128]

    @pl.loop(0, CYCLE)
    def _(step):
        ssend[step] = ssrc[lax.shift_right_logical(pick[step], 2)]

    to_all(scale_copy)

    def x_region(chunk, half, first, second, quarter=None):
        part, low, high = CHUNKS[chunk]
        at = place(first, second) if half == 0 else place(second, first)
        start, size = SHARES[half]
        if quarter is not None:
            size = size // 2
            start += quarter * size
        return xg.at[part, at, pl.ds(start, size), pl.ds(low, high - low)]

    me_at = ((x, y), (y, x))
    ways = (((right, left), (up, down)), ((up, down), (right, left)))

    def x_copy(chunk, half, stage, s, way, receive=False):
        first, second = me_at[half]
        back = (-1 if way == 0 else 1) * (1 if receive else 0)
        on = -1 if way == 0 else 1
        if stage == 0:
            region, axis = x_region(chunk, half, first + back, second), 0
        elif stage == 1:
            region, axis = x_region(chunk, half, first + on + back, second, way), 0
        elif stage == 2:
            region, axis = x_region(chunk, half, first + DELTA[s], second + back), 1
        else:
            region, axis = x_region(chunk, half, first + DELTA[s], second + on + back, way), 1
        arrived = q_recv.at[chunk] if stage == 3 else x_recv.at[chunk, half, (0, 2, 4)[stage] + s * 2 + way]
        return copy(region, region, x_send.at[chunk], arrived, ways[half][axis][way])

    def x_several(chunk, pieces):
        part, low, high = CHUNKS[chunk]
        region = xg.at[part, pl.ds(0, pieces), :, pl.ds(low, high - low)]
        return copy(region, region, x_send.at[chunk], q_recv.at[chunk], right)

    def x_start(chunk, stage, s, way):
        for half in range(2):
            x_copy(chunk, half, stage, s, way).start()

    def x_wait(chunk, half, stage, s, way):
        x_copy(chunk, half, stage, s, way, receive=True).wait_recv()

    gain = gain_ref[...].astype(F32).reshape(1, SLICE)
    lanes = lax.broadcasted_iota(jnp.int32, (HALF, 128), 1) - lax.broadcasted_iota(jnp.int32, (HALF, 128), 0)

    def arrange(chunk):
        part, low, high = CHUNKS[chunk]
        rbuf[chunk][0] = sbuf[chunk][0]
        units(chunk).wait_recv()
        for at in range(UNITS_DEV):
            source = unit_ref[ctx * UNITS_DEV + at]
            slot = (ctx - lax.shift_right_logical(source, 4)) & (CYCLE - 1)
            across = jnp.broadcast_to(srecv[slot], (HALF, 128))
            lane = (source & 3) * UNIT + part * HALF
            scale = jnp.sum(jnp.where(lanes == lane, across, 0.0), -1, keepdims=True)
            rows = rbuf[chunk][slot].astype(F32) * scale * gain[:, low:high]
            xg[part, yh * 8 + head, at * HALF : (at + 1) * HALF, low:high] = rows.astype(BF16)

    def begin(chunk):
        for stage in (0, 2):
            for way in range(2):
                x_start(chunk, stage, 0, way)

    def first_axis(chunk):
        for way in range(2):
            for half in range(2):
                x_wait(chunk, half, 0, 0, way)
                x_copy(chunk, half, 1, 0, way).start()
        for s in (1, 2):
            for way in range(2):
                x_start(chunk, 2, s, way)

    def first_axis_end(chunk):
        for half in range(2):
            for way in range(2):
                x_wait(chunk, half, 1, 0, way)
        for way in range(2):
            x_start(chunk, 2, 3, way)

    def second_axis(chunk, s):
        for way in range(2):
            for half in range(2):
                x_wait(chunk, half, 2, s, way)
                x_copy(chunk, half, 3, s, way).start()

    def second_axis_end(chunk):
        x_several(chunk, 4).wait_recv()

    def w_copy(kind, hop, way, receive=False):
        on = (-1 if way == 0 else 1) * (hop if receive else hop - 1)
        region = weights[kind].at[lax.rem(z + on + NZ, NZ), c]
        sem = (hop - 1) * 2 + way
        return copy(region, region, z_send.at[kind], z_recv.at[kind, sem], (above, below)[way])

    def w_several(kind, pieces, send, recv):
        region = weights[kind].at[pl.ds(0, pieces), 0]
        return copy(region, region, send.at[kind], recv.at[kind], sibling)

    def w_share(kind, at):
        region = weights[kind].at[lax.rem(z + at, NZ), c]
        return copy(region, region, c_send.at[kind], c_recv.at[kind], sibling)

    def w_hop(kind, hop):
        if hop == 1:
            swap_copy(kind, 1 - yh).wait_recv()
            w_share(kind, 0).start()
        for way in range(2):
            last = 3 + way
            if 1 < hop <= last + 1:
                w_copy(kind, hop - 1, way, receive=True).wait_recv()
            if hop <= last:
                w_copy(kind, hop, way).start()
            if 1 < hop <= last + 1:
                w_share(kind, (NZ - (hop - 1)) if way == 0 else hop - 1).start()

    def project(kind, part):
        acc = (acc_kv, acc_q)[kind]

        def one(k):
            w_rows = jnp.concatenate([weights[kind][k, core, row] for row in range(2) for core in range(2)], 0)
            rows = jnp.concatenate([xg[part, k], xg[part, 8 + k]], 0)
            return jnp.dot(rows, w_rows, preferred_element_type=F32)

        acc[...] = one(0)

        @pl.loop(1, 8)
        def _(k):
            acc[...] += one(k)

    def turn(value, part, row):
        places = slice(part * 16, (part + 1) * 16)
        cos_at, sin_at = cosine[row, places].reshape(ROWS, 128), sine[row, places].reshape(ROWS, 128)
        return value * cos_at + pltpu.roll(value, HEAD_DIM // 2, 1) * sin_at

    def halo(which, part, receive=False):
        if which == 0:
            src, dst, to = 5 + c, 1 + c, above
        elif which == 1:
            src, dst, to = 1 + c, 2 - c if receive else 1 + c, sibling
        elif which == 2:
            src, dst, to = 3 + c, 4 - c if receive else 3 + c, sibling
        elif which == 3:
            src, dst, to = 5, 5, sibling
        else:
            src, dst, to = 4, 0, device(x, y, z + 1, 0)
        return copy(
            kvb.at[src, part], kvb.at[dst, part], h_send.at[which, part], h_recv.at[which, part], to
        )

    def project_keys_values(part, row):
        acc = acc_kv.at[row * ROWS : (row + 1) * ROWS]

        def one(k):
            w_rows = jnp.concatenate([wkv[k, core, half] for half in range(2) for core in range(2)], 0)
            return jnp.dot(xg[part, 8 * row + k], w_rows, preferred_element_type=F32)

        acc[...] = one(0)

        @pl.loop(1, 8)
        def _(k):
            acc[...] += one(k)

    def keys_values(part):
        if part == 0:
            project(0, part)
        for row in (1, 0):
            if part == 1:
                project_keys_values(part, row)
            at = 2 * row + 3 + c
            rows = slice(row * ROWS, (row + 1) * ROWS)
            for side in range(2):
                keys = acc_kv[rows, side * 128 : (side + 1) * 128]
                vals = acc_kv[rows, 256 + side * 128 : 256 + (side + 1) * 128]
                kvb[at, part, side, 0] = turn(keys, part, row).astype(BF16)
                kvb[at, part, side, 1] = vals.astype(BF16)
            if row == 1:
                halo(0, part).start()

                @pl.when(c == 0)
                def _():
                    halo(3, part).start()

            else:

                @pl.when(c == 1)
                def _():
                    halo(4, part).start()

                halo(2, part).start()

    def queries(part):
        project(1, part)
        for row in range(2):
            rows = slice(row * ROWS, (row + 1) * ROWS)
            for side in range(2):
                query = acc_q[rows, side * 128 : (side + 1) * 128]
                qb[row, side, part] = turn(query, part, row).astype(BF16)

    def pass_on(part):
        halo(0, part, receive=True).wait_recv()
        halo(1, part).start()

    def block_of(at, side, kind):
        return kvb[at, :, side, kind].reshape(BLOCK, HEAD_DIM)

    def attend(row, side, tile, lags, first):
        query = qb[row, side, tile]
        own = 2 * row + 3 + c
        block = (z * 4 + 2 * row + c + CYCLE - first_ref[0]) & (CYCLE - 1)
        pieces = []
        for lag in lags:
            keys = block_of(own - lag, side, 0)
            value = lax.dot_general(query, keys, (((1,), (1,)), ((), ())), preferred_element_type=F32) * BASE2
            if lag == 0:
                pieces.append((value + unseen[tile], 0.0, own))
            else:
                pieces.append((value, jnp.where(block >= lag, 0.0, -1e30).astype(F32), own - lag))
        peak = None
        for value, bias, _ in pieces:
            top = jnp.max(value, -1, keepdims=True) + bias
            peak = top if peak is None else jnp.maximum(peak, top)
        if not first:
            before = mrow[row, side, tile, :, :1]
            peak = jnp.maximum(peak, before)
        total, summed = None, None
        for value, bias, at in pieces:
            weight = jnp.exp2(value - (peak - bias))
            part_total = jnp.sum(weight, -1, keepdims=True)
            part_sum = jnp.dot(weight.astype(BF16), block_of(at, side, 1), preferred_element_type=F32)
            total = part_total if total is None else total + part_total
            summed = part_sum if summed is None else summed + part_sum
        if not first:
            keep = jnp.exp2(before - peak)
            total = total + lrow[row, side, tile, :, :1] * keep
            summed = summed + att[row, side, tile] * keep
        return peak, total, summed

    def attend_some(row, side, lags, first=False):
        for tile in range(2):
            peak, total, summed = attend(row, side, tile, lags, first)
            mrow[row, side, tile] = jnp.broadcast_to(peak, (ROWS, 128))
            lrow[row, side, tile] = jnp.broadcast_to(total, (ROWS, 128))
            att[row, side, tile] = summed

    def attend_last(row, side, lags):
        for tile in range(2):
            _, total, summed = attend(row, side, tile, lags, False)
            obuf[row, side, :, tile] = (summed / total).astype(BF16).reshape(UNITS_DEV, HALF, HEAD_DIM)

    def out_copy(row, side):
        return copy(obuf.at[row, side], oswap.at[side], o_send.at[side], o_recv.at[side], partner)

    srecv[0] = ssend[0]
    send_units(1)
    w_hop(0, 1)
    scales().wait_recv()
    arrange(0)
    begin(0)
    send_units(2)
    first_axis(0)
    w_hop(1, 1)
    arrange(1)
    begin(1)
    first_axis_end(0)
    w_hop(0, 2)
    second_axis(0, 0)
    first_axis(1)
    second_axis(0, 1)
    second_axis(0, 2)
    first_axis_end(1)
    second_axis(0, 3)
    w_hop(0, 3)
    second_axis(1, 0)
    second_axis(1, 1)
    second_axis_end(0)
    w_hop(1, 2)
    arrange(2)
    begin(2)
    second_axis(1, 2)
    second_axis(1, 3)
    w_hop(0, 4)
    second_axis_end(1)
    first_axis(2)
    first_axis_end(2)
    w_hop(0, 5)
    second_axis(2, 0)
    w_hop(1, 3)
    w_several(0, 8, c_send, c_recv).wait_recv()
    keys_values(0)
    second_axis(2, 1)
    w_hop(1, 4)
    second_axis(2, 2)
    second_axis(2, 3)
    w_hop(1, 5)
    w_several(1, 8, c_send, c_recv).wait_recv()
    queries(0)
    pass_on(0)
    second_axis_end(2)
    keys_values(1)
    queries(1)
    for part in range(2):
        halo(2, part, receive=True).wait_recv()

        @pl.when(c == 1)
        def _(part=part):
            halo(3, part).wait_recv()

    for side in range(2):
        attend_some(1, side, (0, 1, 2), True)
        attend_some(0, side, (0,), True)
    pass_on(1)
    for part in range(2):
        halo(1, part, receive=True).wait_recv()
    @pl.when(yh == 0)
    def _():
        for side in range(2):
            attend_last(1, side, (3,))
            out_copy(1, side).start()

    for side in range(2):
        attend_some(0, side, (1, 2))
    for part in range(2):

        @pl.when(c == 0)
        def _(part=part):
            halo(4, part).wait_recv()

    for side in range(2):
        attend_last(0, side, (3,))

        @pl.when(yh == 1)
        def _(side=side):
            out_copy(0, side).start()

    @pl.when(yh == 1)
    def _():
        for side in range(2):
            attend_last(1, side, (3,))

    for side in range(2):
        out_ref[2 * yh + side] = obuf[yh, side].reshape(BLOCK, HEAD_DIM)
    for side in range(2):
        out_copy(yh, side).wait_recv()
        out_ref[2 - 2 * yh + side] = oswap[side].reshape(BLOCK, HEAD_DIM)

    sums_of_others().wait_send()
    scales().wait_send()
    for chunk in range(n):
        units(chunk).wait_send()
        x_several(chunk, 15).wait_send()
    for kind in range(2):
        swap_copy(kind, yh).wait_send()
        w_several(kind, 7, z_send, c_recv).wait_send()
        w_several(kind, 8, c_send, c_recv).wait_send()
    for part in range(2):
        for which in range(3):
            halo(which, part).wait_send()

        @pl.when(c == 0)
        def _(part=part):
            halo(3, part).wait_send()

        @pl.when(c == 1)
        def _(part=part):
            halo(4, part).wait_send()

    for side in range(2):
        out_copy(1 - yh, side).wait_send()


def per_device(latents, norm_gain, w_qkv, source_unit, first_block):
    half = HEAD_DIM // 2
    freq = np.exp(-math.log(ROPE_BASE) * np.arange(half) * (2.0 / HEAD_DIM))
    freq = np.concatenate([freq, freq])
    sign = np.concatenate([-np.ones(half), np.ones(half)])

    def table(positions):
        angles = np.asarray(positions)[:, None] * freq
        return np.stack([np.cos(angles), np.sin(angles) * sign]).astype(np.float32)

    base = table(np.concatenate([np.arange(CYCLE) * BLOCK, np.arange(32) * 16]))[:, :, None]
    near = table(np.arange(16))
    smem, vmem = pl.BlockSpec(memory_space=pltpu.SMEM), pl.BlockSpec(memory_space=pltpu.VMEM)
    dma = pltpu.SemaphoreType.DMA
    unit_slots = [pltpu.VMEM((CYCLE, HALF, high - low), BF16) for _, low, high in CHUNKS]
    n = len(CHUNKS)
    out = pl.pallas_call(
        kernel,
        out_shape=jax.ShapeDtypeStruct((4, BLOCK, HEAD_DIM), BF16),
        in_specs=[smem] * 2 + [vmem] * 5,
        out_specs=vmem,
        scratch_shapes=unit_slots
        + unit_slots
        + [
            pltpu.SMEM((CYCLE,), jnp.int32),
            pltpu.VMEM((4, 1, 128), F32),
            pltpu.VMEM((CYCLE, 1, 128), F32),
            pltpu.VMEM((CYCLE, 1, 128), F32),
            pltpu.VMEM((2, 16, ROWS, SLICE), BF16),
            pltpu.VMEM((1, BLOCK), F32),
            pltpu.VMEM((8, 1, BLOCK), F32),
            pltpu.VMEM((2, 128, 512), BF16),
            pltpu.VMEM((2, 128, 256), BF16),
            pltpu.VMEM((NZ, 2, 2, 128, 512), BF16),
            pltpu.VMEM((NZ, 2, 2, 128, 256), BF16),
            pltpu.VMEM((2 * ROWS, 512), F32),
            pltpu.VMEM((2 * ROWS, 256), F32),
            pltpu.VMEM((7, 2, 2, 2, ROWS, HEAD_DIM), BF16),
            pltpu.VMEM((2, 2, 2, ROWS, HEAD_DIM), BF16),
            pltpu.VMEM((2, ROWS, BLOCK), F32),
            pltpu.VMEM((2, 32, 16, 128), F32),
            pltpu.VMEM((2, 32, 16, 128), F32),
            pltpu.VMEM((2, 2, 2, ROWS, HEAD_DIM), F32),
            pltpu.VMEM((2, 2, 2, ROWS, 128), F32),
            pltpu.VMEM((2, 2, 2, ROWS, 128), F32),
            pltpu.VMEM((2, 2, UNITS_DEV, 2, HALF, HEAD_DIM), BF16),
            pltpu.VMEM((2, UNITS_DEV, 2, HALF, HEAD_DIM), BF16),
            dma((n,)), dma((n,)),
            dma((1,)), dma((1,)),
            dma((1,)), dma((1,)),
            dma((n,)), dma((n, 2, 12)), dma((n,)),
            dma((2,)), dma((2,)),
            dma((2,)), dma((2, 8)),
            dma((2,)), dma((2,)),
            dma((5, 2)), dma((5, 2)),
            dma((2,)), dma((2,)),
        ],
        compiler_params=pltpu.CompilerParams(
            collective_id=0, has_side_effects=True, vmem_limit_bytes=56 * 1024 * 1024
        ),
    )(
        source_unit, first_block, latents.reshape(UNITS_DEV, UNIT, SLICE), norm_gain,
        w_qkv, base, near,
    )
    return jnp.transpose(out, (1, 0, 2))


def solution(mesh):
    placed = (P("ctx", "head"), P("head"), P("ctx", "head", None), P(), P())
    return jax.shard_map(
        per_device, mesh=mesh, in_specs=placed, out_specs=P("ctx", "head", None), check_vma=False
    )
```

```python
import math

import jax
import jax.numpy as jnp
import numpy as np
from jax import lax
from jax.experimental import pallas as pl
from jax.experimental.pallas import tpu as pltpu
from jax.sharding import PartitionSpec as P

HEAD_DIM = 128
UNITS_DEV = 16
STEPS = 4
EPS = 1e-05
ROPE_BASE = 50000000.0

BLOCK = 512
UNIT = BLOCK // UNITS_DEV
SLICE = 512
HALF = UNIT // 2
ROWS = BLOCK // 2
NZ, NY, NX = 8, 4, 4
CYCLE = 32
WIDTH = 4096
MESH = pl.DeviceIdType.MESH
F32, BF16 = jnp.float32, jnp.bfloat16
DELTA = (0, -1, 1, 2)
CHUNKS = ((0, 0, 256), (0, 256, 512), (1, 0, 512))
SHARES = ((0, 128), (128, 128))
BASE2 = math.log2(math.e) * HEAD_DIM**-0.5


def kernel(*refs):
    unit_ref, first_ref, lat_ref, gain_ref, w_ref, base_ref, near_ref, out_ref = refs[:8]
    refs = refs[8:]
    n = len(CHUNKS)
    sbuf, rbuf, refs = refs[:n], refs[n : 2 * n], refs[2 * n :]
    (pick, ssrc, ssend, srecv, xg, own_sum, all_sums, wstage_kv, wstage_q, wkv, wq, acc_kv, acc_q, kvb, qb,
     unseen, cosine, sine, att, mrow, lrow, obuf, oswap,
     a_send, a_recv, s_send, s_recv, g_send, g_recv, x_send, x_recv, q_recv, y_send, y_recv, z_send, z_recv,
     c_send, c_recv, h_send, h_recv, o_send, o_recv) = refs
    ctx, head = lax.axis_index("ctx"), lax.axis_index("head")
    z, yh, c = ctx // 4, (ctx // 2) % 2, ctx % 2
    yl, x = head // 4, head % 4
    y = yh * 2 + yl

    def place(at_x, at_y):
        return lax.rem(at_y + 4, 4) * 4 + lax.rem(at_x + 4, 4)

    def device(at_x, at_y, at_z, at_c):
        at = place(at_x, at_y)
        return (lax.rem(at_z + NZ, NZ) * 4 + at // 8 * 2 + at_c, lax.rem(at, 8))

    right, left = device(x + 1, y, z, c), device(x - 1, y, z, c)
    up, down = device(x, y + 1, z, c), device(x, y - 1, z, c)
    above, below = device(x, y, z + 1, c), device(x, y, z - 1, c)
    sibling = device(x, y, z, 1 - c)
    partner = device(x, y + 2, z, c)

    def copy(src, dst, send, recv, to):
        return pltpu.make_async_remote_copy(
            src_ref=src, dst_ref=dst, send_sem=send, recv_sem=recv, device_id=to, device_id_type=MESH
        )

    barrier = pltpu.get_barrier_semaphore()

    @pl.loop(1, CYCLE)
    def _(step):
        pl.semaphore_signal(barrier, inc=1, device_id=(lax.rem(ctx + step, CYCLE), head), device_id_type=MESH)

    @pl.loop(1, 8)
    def _(step):
        pl.semaphore_signal(barrier, inc=1, device_id=(ctx, lax.rem(head + step, 8)), device_id_type=MESH)

    for to in (up, down):
        pl.semaphore_signal(barrier, inc=1, device_id=to, device_id_type=MESH)

    @pl.loop(0, CYCLE)
    def _(step):
        start = lax.rem(ctx + step, CYCLE) * UNITS_DEV
        chosen = jnp.int32(0)
        for at in range(UNITS_DEV):
            value = unit_ref[start + at]
            chosen = chosen + jnp.where(lax.shift_right_logical(value, 4) == ctx, value & 15, 0)
        pick[step] = chosen

    def fill(chunk):
        part, low, high = CHUNKS[chunk]

        @pl.loop(0, CYCLE)
        def _(step):
            sbuf[chunk][step] = lat_ref[pick[step], part * HALF : (part + 1) * HALF, low:high]

    fill(0)

    eye = lax.broadcasted_iota(jnp.int32, (128, 128), 0) == lax.broadcasted_iota(jnp.int32, (128, 128), 1)
    for at in range(4):
        rows = lat_ref[at * 4 : (at + 1) * 4].astype(F32).reshape(128, SLICE)
        sums = jnp.sum(rows * rows, -1, keepdims=True)
        own_sum[:, at * 128 : (at + 1) * 128] = jnp.sum(jnp.where(eye, sums, 0.0), 0, keepdims=True)
    all_sums[head] = own_sum[...]

    pl.semaphore_wait(barrier, CYCLE - 1 + 7 + 2)

    def sum_copy(step):
        return copy(
            own_sum, all_sums.at[head], g_send.at[0], g_recv.at[0], (ctx, lax.rem(head + step, 8))
        )

    def sums_of_others():
        others = all_sums.at[pl.ds(0, 7)]
        return copy(others, others, g_send.at[0], g_recv.at[0], sibling)

    @pl.loop(1, 8)
    def _(step):
        sum_copy(step).start()

    def unit_copy(chunk, step):
        return copy(
            sbuf[chunk].at[step], rbuf[chunk].at[step], a_send.at[chunk], a_recv.at[chunk],
            (lax.rem(ctx + step, CYCLE), head),
        )

    def units(chunk):
        others = pl.ds(1, CYCLE - 1)
        return copy(
            sbuf[chunk].at[others], rbuf[chunk].at[others], a_send.at[chunk], a_recv.at[chunk], sibling
        )

    def scale_copy(step):
        return copy(ssend.at[step], srecv.at[step], s_send.at[0], s_recv.at[0], (lax.rem(ctx + step, CYCLE), head))

    def scales():
        others = pl.ds(1, CYCLE - 1)
        return copy(ssend.at[others], srecv.at[others], s_send.at[0], s_recv.at[0], sibling)

    def to_all(one):
        @pl.loop(1, CYCLE // 2)
        def _(step):
            one(step).start()
            one(CYCLE - step).start()

        one(CYCLE // 2).start()

    def send_units(chunk):
        to_all(lambda step: unit_copy(chunk, step))

    send_units(0)

    for at in range(4):
        pair, side = at // 2, at % 2
        wstage_q[pair, :, side * 128 : (side + 1) * 128] = w_ref[:, at, :128]
        wstage_kv[pair, :, side * 128 : (side + 1) * 128] = w_ref[:, at, 128:256]
        wstage_kv[pair, :, 256 + side * 128 : 256 + (side + 1) * 128] = w_ref[:, at, 256:]
    stages, weights = (wstage_kv, wstage_q), (wkv, wq)

    def swap_copy(kind, row):
        return copy(
            stages[kind].at[1 - row], weights[kind].at[z, c, row], y_send.at[kind], y_recv.at[kind], partner
        )

    for kind in range(2):
        swap_copy(kind, yh).start()
        weights[kind][z, c, yh] = stages[kind][yh]

    for chunk in range(1, n):
        fill(chunk)

    for part in range(2):
        row_at = lax.broadcasted_iota(jnp.int32, (ROWS, BLOCK), 0)
        key_at = lax.broadcasted_iota(jnp.int32, (ROWS, BLOCK), 1)
        row_pos = (row_at & ~15) * 2 + part * HALF + (row_at & 15)
        key_part = jnp.where(key_at >= ROWS, 1, 0)
        key_low = key_at - key_part * ROWS
        key_pos = (key_low & ~15) * 2 + key_part * HALF + (key_low & 15)
        unseen[part] = jnp.where(row_pos >= key_pos, 0.0, -1e30).astype(F32)

    for row in range(2):
        block = (z * 4 + 2 * row + c + CYCLE - first_ref[0]) & (CYCLE - 1)
        base_cos, base_sin = base_ref[0, block], base_ref[1, block]

        @pl.loop(0, 32)
        def _(at, row=row, base_cos=base_cos, base_sin=base_sin):
            step_cos, step_sin = base_ref[0, CYCLE + at], base_ref[1, CYCLE + at]
            far_cos = base_cos * step_cos - base_sin * step_sin
            far_sin = base_sin * step_cos + base_cos * step_sin
            near_cos, near_sin = near_ref[0], near_ref[1]
            to = lax.rem(at, 2) * 16 + at // 2
            cosine[row, to] = far_cos * near_cos - far_sin * near_sin
            sine[row, to] = far_sin * near_cos + far_cos * near_sin

    sums_of_others().wait_recv()

    inverse = lax.rsqrt(jnp.sum(all_sums[...], 0) / WIDTH + EPS)
    for at in range(4):
        ssrc[at] = inverse[:, at * 128 : (at + 1) * 128]

    @pl.loop(0, CYCLE)
    def _(step):
        ssend[step] = ssrc[lax.shift_right_logical(pick[step], 2)]

    to_all(scale_copy)

    def x_region(chunk, half, first, second, quarter=None):
        part, low, high = CHUNKS[chunk]
        at = place(first, second) if half == 0 else place(second, first)
        start, size = SHARES[half]
        if quarter is not None:
            size = size // 2
            start += quarter * size
        return xg.at[part, at, pl.ds(start, size), pl.ds(low, high - low)]

    me_at = ((x, y), (y, x))
    ways = (((right, left), (up, down)), ((up, down), (right, left)))

    def x_copy(chunk, half, stage, s, way, receive=False):
        first, second = me_at[half]
        back = (-1 if way == 0 else 1) * (1 if receive else 0)
        on = -1 if way == 0 else 1
        if stage == 0:
            region, axis = x_region(chunk, half, first + back, second), 0
        elif stage == 1:
            region, axis = x_region(chunk, half, first + on + back, second, way), 0
        elif stage == 2:
            region, axis = x_region(chunk, half, first + DELTA[s], second + back), 1
        else:
            region, axis = x_region(chunk, half, first + DELTA[s], second + on + back, way), 1
        arrived = q_recv.at[chunk] if stage == 3 else x_recv.at[chunk, half, (0, 2, 4)[stage] + s * 2 + way]
        return copy(region, region, x_send.at[chunk], arrived, ways[half][axis][way])

    def x_several(chunk, pieces):
        part, low, high = CHUNKS[chunk]
        region = xg.at[part, pl.ds(0, pieces), :, pl.ds(low, high - low)]
        return copy(region, region, x_send.at[chunk], q_recv.at[chunk], right)

    def x_start(chunk, stage, s, way):
        for half in range(2):
            x_copy(chunk, half, stage, s, way).start()

    def x_wait(chunk, half, stage, s, way):
        x_copy(chunk, half, stage, s, way, receive=True).wait_recv()

    gain = gain_ref[...].astype(F32).reshape(1, SLICE)
    lanes = lax.broadcasted_iota(jnp.int32, (HALF, 128), 1) - lax.broadcasted_iota(jnp.int32, (HALF, 128), 0)

    def arrange(chunk):
        part, low, high = CHUNKS[chunk]
        rbuf[chunk][0] = sbuf[chunk][0]
        units(chunk).wait_recv()
        for at in range(UNITS_DEV):
            source = unit_ref[ctx * UNITS_DEV + at]
            slot = (ctx - lax.shift_right_logical(source, 4)) & (CYCLE - 1)
            across = jnp.broadcast_to(srecv[slot], (HALF, 128))
            lane = (source & 3) * UNIT + part * HALF
            scale = jnp.sum(jnp.where(lanes == lane, across, 0.0), -1, keepdims=True)
            rows = rbuf[chunk][slot].astype(F32) * scale * gain[:, low:high]
            xg[part, yh * 8 + head, at * HALF : (at + 1) * HALF, low:high] = rows.astype(BF16)

    def begin(chunk):
        for stage in (0, 2):
            for way in range(2):
                x_start(chunk, stage, 0, way)

    def first_axis(chunk):
        for way in range(2):
            for half in range(2):
                x_wait(chunk, half, 0, 0, way)
                x_copy(chunk, half, 1, 0, way).start()
        for s in (1, 2):
            for way in range(2):
                x_start(chunk, 2, s, way)

    def first_axis_end(chunk):
        for half in range(2):
            for way in range(2):
                x_wait(chunk, half, 1, 0, way)
        for way in range(2):
            x_start(chunk, 2, 3, way)

    def second_axis(chunk, s):
        for way in range(2):
            for half in range(2):
                x_wait(chunk, half, 2, s, way)
                x_copy(chunk, half, 3, s, way).start()

    def second_axis_end(chunk):
        x_several(chunk, 4).wait_recv()

    def w_copy(kind, hop, way, receive=False):
        on = (-1 if way == 0 else 1) * (hop if receive else hop - 1)
        region = weights[kind].at[lax.rem(z + on + NZ, NZ), c]
        sem = (hop - 1) * 2 + way
        return copy(region, region, z_send.at[kind], z_recv.at[kind, sem], (above, below)[way])

    def w_several(kind, pieces, send, recv):
        region = weights[kind].at[pl.ds(0, pieces), 0]
        return copy(region, region, send.at[kind], recv.at[kind], sibling)

    def w_share(kind, at):
        region = weights[kind].at[lax.rem(z + at, NZ), c]
        return copy(region, region, c_send.at[kind], c_recv.at[kind], sibling)

    def w_hop(kind, hop):
        if hop == 1:
            swap_copy(kind, 1 - yh).wait_recv()
            w_share(kind, 0).start()
        for way in range(2):
            last = 3 + way
            if 1 < hop <= last + 1:
                w_copy(kind, hop - 1, way, receive=True).wait_recv()
            if hop <= last:
                w_copy(kind, hop, way).start()
            if 1 < hop <= last + 1:
                w_share(kind, (NZ - (hop - 1)) if way == 0 else hop - 1).start()

    def project(kind, part):
        acc = (acc_kv, acc_q)[kind]

        def one(k):
            w_rows = jnp.concatenate([weights[kind][k, core, row] for row in range(2) for core in range(2)], 0)
            rows = jnp.concatenate([xg[part, k], xg[part, 8 + k]], 0)
            return jnp.dot(rows, w_rows, preferred_element_type=F32)

        acc[...] = one(0)

        @pl.loop(1, 8)
        def _(k):
            acc[...] += one(k)

    def turn(value, part, row):
        places = slice(part * 16, (part + 1) * 16)
        cos_at, sin_at = cosine[row, places].reshape(ROWS, 128), sine[row, places].reshape(ROWS, 128)
        return value * cos_at + pltpu.roll(value, HEAD_DIM // 2, 1) * sin_at

    def halo(which, part, receive=False):
        if which == 0:
            src, dst, to = 5 + c, 1 + c, above
        elif which == 1:
            src, dst, to = 1 + c, 2 - c if receive else 1 + c, sibling
        elif which == 2:
            src, dst, to = 3 + c, 4 - c if receive else 3 + c, sibling
        elif which == 3:
            src, dst, to = 5, 5, sibling
        else:
            src, dst, to = 4, 0, device(x, y, z + 1, 0)
        return copy(
            kvb.at[src, part], kvb.at[dst, part], h_send.at[which, part], h_recv.at[which, part], to
        )

    def project_keys_values(part, row):
        acc = acc_kv.at[row * ROWS : (row + 1) * ROWS]

        def one(k):
            w_rows = jnp.concatenate([wkv[k, core, half] for half in range(2) for core in range(2)], 0)
            return jnp.dot(xg[part, 8 * row + k], w_rows, preferred_element_type=F32)

        acc[...] = one(0)

        @pl.loop(1, 8)
        def _(k):
            acc[...] += one(k)

    def keys_values(part):
        if part == 0:
            project(0, part)
        for row in (1, 0):
            if part == 1:
                project_keys_values(part, row)
            at = 2 * row + 3 + c
            rows = slice(row * ROWS, (row + 1) * ROWS)
            for side in range(2):
                keys = acc_kv[rows, side * 128 : (side + 1) * 128]
                vals = acc_kv[rows, 256 + side * 128 : 256 + (side + 1) * 128]
                kvb[at, part, side, 0] = turn(keys, part, row).astype(BF16)
                kvb[at, part, side, 1] = vals.astype(BF16)
            if row == 1:
                halo(0, part).start()

                @pl.when(c == 0)
                def _():
                    halo(3, part).start()

            else:

                @pl.when(c == 1)
                def _():
                    halo(4, part).start()

                halo(2, part).start()

    def queries(part):
        project(1, part)
        for row in range(2):
            rows = slice(row * ROWS, (row + 1) * ROWS)
            for side in range(2):
                query = acc_q[rows, side * 128 : (side + 1) * 128]
                qb[row, side, part] = turn(query, part, row).astype(BF16)

    def pass_on(part):
        halo(0, part, receive=True).wait_recv()
        halo(1, part).start()

    def block_of(at, side, kind):
        return kvb[at, :, side, kind].reshape(BLOCK, HEAD_DIM)

    def attend(row, side, tile, lags, first):
        query = qb[row, side, tile]
        own = 2 * row + 3 + c
        block = (z * 4 + 2 * row + c + CYCLE - first_ref[0]) & (CYCLE - 1)
        pieces = []
        for lag in lags:
            keys = block_of(own - lag, side, 0)
            value = lax.dot_general(query, keys, (((1,), (1,)), ((), ())), preferred_element_type=F32) * BASE2
            if lag == 0:
                pieces.append((value + unseen[tile], 0.0, own))
            else:
                pieces.append((value, jnp.where(block >= lag, 0.0, -1e30).astype(F32), own - lag))
        peak = None
        for value, bias, _ in pieces:
            top = jnp.max(value, -1, keepdims=True) + bias
            peak = top if peak is None else jnp.maximum(peak, top)
        if not first:
            before = mrow[row, side, tile, :, :1]
            peak = jnp.maximum(peak, before)
        total, summed = None, None
        for value, bias, at in pieces:
            weight = jnp.exp2(value - (peak - bias))
            part_total = jnp.sum(weight, -1, keepdims=True)
            part_sum = jnp.dot(weight.astype(BF16), block_of(at, side, 1), preferred_element_type=F32)
            total = part_total if total is None else total + part_total
            summed = part_sum if summed is None else summed + part_sum
        if not first:
            keep = jnp.exp2(before - peak)
            total = total + lrow[row, side, tile, :, :1] * keep
            summed = summed + att[row, side, tile] * keep
        return peak, total, summed

    def attend_some(row, side, lags, first=False):
        for tile in range(2):
            peak, total, summed = attend(row, side, tile, lags, first)
            mrow[row, side, tile] = jnp.broadcast_to(peak, (ROWS, 128))
            lrow[row, side, tile] = jnp.broadcast_to(total, (ROWS, 128))
            att[row, side, tile] = summed

    def attend_last(row, side, lags):
        for tile in range(2):
            _, total, summed = attend(row, side, tile, lags, False)
            obuf[row, side, :, tile] = (summed / total).astype(BF16).reshape(UNITS_DEV, HALF, HEAD_DIM)

    def out_copy(row, side):
        return copy(obuf.at[row, side], oswap.at[side], o_send.at[side], o_recv.at[side], partner)

    srecv[0] = ssend[0]
    w_hop(0, 1)
    send_units(1)
    scales().wait_recv()
    arrange(0)
    begin(0)
    send_units(2)
    first_axis(0)
    w_hop(1, 1)
    arrange(1)
    begin(1)
    first_axis_end(0)
    w_hop(0, 2)
    second_axis(0, 0)
    first_axis(1)
    second_axis(0, 1)
    second_axis(0, 2)
    first_axis_end(1)
    second_axis(0, 3)
    w_hop(0, 3)
    second_axis(1, 0)
    second_axis(1, 1)
    second_axis_end(0)
    w_hop(1, 2)
    arrange(2)
    begin(2)
    second_axis(1, 2)
    second_axis(1, 3)
    w_hop(0, 4)
    second_axis_end(1)
    first_axis(2)
    first_axis_end(2)
    w_hop(0, 5)
    second_axis(2, 0)
    w_hop(1, 3)
    w_several(0, 8, c_send, c_recv).wait_recv()
    keys_values(0)
    second_axis(2, 1)
    w_hop(1, 4)
    second_axis(2, 2)
    second_axis(2, 3)
    w_hop(1, 5)
    w_several(1, 8, c_send, c_recv).wait_recv()
    queries(0)
    pass_on(0)
    second_axis_end(2)
    keys_values(1)
    queries(1)
    for part in range(2):
        halo(2, part, receive=True).wait_recv()

        @pl.when(c == 1)
        def _(part=part):
            halo(3, part).wait_recv()

    for side in range(2):
        attend_some(1, side, (0, 1, 2), True)
        attend_some(0, side, (0,), True)
    pass_on(1)
    for part in range(2):
        halo(1, part, receive=True).wait_recv()
    @pl.when(yh == 0)
    def _():
        for side in range(2):
            attend_last(1, side, (3,))
            out_copy(1, side).start()

    for side in range(2):
        attend_some(0, side, (1, 2))
    for part in range(2):

        @pl.when(c == 0)
        def _(part=part):
            halo(4, part).wait_recv()

    for side in range(2):
        attend_last(0, side, (3,))

        @pl.when(yh == 1)
        def _(side=side):
            out_copy(0, side).start()

    @pl.when(yh == 1)
    def _():
        for side in range(2):
            attend_last(1, side, (3,))

    for side in range(2):
        out_ref[2 * yh + side] = obuf[yh, side].reshape(BLOCK, HEAD_DIM)
    for side in range(2):
        out_copy(yh, side).wait_recv()
        out_ref[2 - 2 * yh + side] = oswap[side].reshape(BLOCK, HEAD_DIM)

    sums_of_others().wait_send()
    scales().wait_send()
    for chunk in range(n):
        units(chunk).wait_send()
        x_several(chunk, 15).wait_send()
    for kind in range(2):
        swap_copy(kind, yh).wait_send()
        w_several(kind, 7, z_send, c_recv).wait_send()
        w_several(kind, 8, c_send, c_recv).wait_send()
    for part in range(2):
        for which in range(3):
            halo(which, part).wait_send()

        @pl.when(c == 0)
        def _(part=part):
            halo(3, part).wait_send()

        @pl.when(c == 1)
        def _(part=part):
            halo(4, part).wait_send()

    for side in range(2):
        out_copy(1 - yh, side).wait_send()


def per_device(latents, norm_gain, w_qkv, source_unit, first_block):
    half = HEAD_DIM // 2
    freq = np.exp(-math.log(ROPE_BASE) * np.arange(half) * (2.0 / HEAD_DIM))
    freq = np.concatenate([freq, freq])
    sign = np.concatenate([-np.ones(half), np.ones(half)])

    def table(positions):
        angles = np.asarray(positions)[:, None] * freq
        return np.stack([np.cos(angles), np.sin(angles) * sign]).astype(np.float32)

    base = table(np.concatenate([np.arange(CYCLE) * BLOCK, np.arange(32) * 16]))[:, :, None]
    near = table(np.arange(16))
    smem, vmem = pl.BlockSpec(memory_space=pltpu.SMEM), pl.BlockSpec(memory_space=pltpu.VMEM)
    dma = pltpu.SemaphoreType.DMA
    unit_slots = [pltpu.VMEM((CYCLE, HALF, high - low), BF16) for _, low, high in CHUNKS]
    n = len(CHUNKS)
    out = pl.pallas_call(
        kernel,
        out_shape=jax.ShapeDtypeStruct((4, BLOCK, HEAD_DIM), BF16),
        in_specs=[smem] * 2 + [vmem] * 5,
        out_specs=vmem,
        scratch_shapes=unit_slots
        + unit_slots
        + [
            pltpu.SMEM((CYCLE,), jnp.int32),
            pltpu.VMEM((4, 1, 128), F32),
            pltpu.VMEM((CYCLE, 1, 128), F32),
            pltpu.VMEM((CYCLE, 1, 128), F32),
            pltpu.VMEM((2, 16, ROWS, SLICE), BF16),
            pltpu.VMEM((1, BLOCK), F32),
            pltpu.VMEM((8, 1, BLOCK), F32),
            pltpu.VMEM((2, 128, 512), BF16),
            pltpu.VMEM((2, 128, 256), BF16),
            pltpu.VMEM((NZ, 2, 2, 128, 512), BF16),
            pltpu.VMEM((NZ, 2, 2, 128, 256), BF16),
            pltpu.VMEM((2 * ROWS, 512), F32),
            pltpu.VMEM((2 * ROWS, 256), F32),
            pltpu.VMEM((7, 2, 2, 2, ROWS, HEAD_DIM), BF16),
            pltpu.VMEM((2, 2, 2, ROWS, HEAD_DIM), BF16),
            pltpu.VMEM((2, ROWS, BLOCK), F32),
            pltpu.VMEM((2, 32, 16, 128), F32),
            pltpu.VMEM((2, 32, 16, 128), F32),
            pltpu.VMEM((2, 2, 2, ROWS, HEAD_DIM), F32),
            pltpu.VMEM((2, 2, 2, ROWS, 128), F32),
            pltpu.VMEM((2, 2, 2, ROWS, 128), F32),
            pltpu.VMEM((2, 2, UNITS_DEV, 2, HALF, HEAD_DIM), BF16),
            pltpu.VMEM((2, UNITS_DEV, 2, HALF, HEAD_DIM), BF16),
            dma((n,)), dma((n,)),
            dma((1,)), dma((1,)),
            dma((1,)), dma((1,)),
            dma((n,)), dma((n, 2, 12)), dma((n,)),
            dma((2,)), dma((2,)),
            dma((2,)), dma((2, 8)),
            dma((2,)), dma((2,)),
            dma((5, 2)), dma((5, 2)),
            dma((2,)), dma((2,)),
        ],
        compiler_params=pltpu.CompilerParams(
            collective_id=0, has_side_effects=True, vmem_limit_bytes=56 * 1024 * 1024
        ),
    )(
        source_unit, first_block, latents.reshape(UNITS_DEV, UNIT, SLICE), norm_gain,
        w_qkv, base, near,
    )
    return jnp.transpose(out, (1, 0, 2))


def solution(mesh):
    placed = (P("ctx", "head"), P("head"), P("ctx", "head", None), P(), P())
    return jax.shard_map(
        per_device, mesh=mesh, in_specs=placed, out_specs=P("ctx", "head", None), check_vma=False
    )
```
